32 devices in a mesh: scen: 2 (over x), lx: 4 (over y, core), ly: 4 (over z).
Axes of the slice: x: 2, y: 2, z: 4, core: 2. Of those that a mesh axis runs over, the one named last changes fastest.
Arguments:
- density: float32 [2, 512, 2048], P('scen', 'lx', 'ly'), may hold values from 0.2 to 1.5
- trait: float32 [2, 512, 2048], P('scen', 'lx', 'ly'), may hold values from -4 to 4
- variance: float32 [2, 512, 2048], P('scen', 'lx', 'ly'), may hold values from 0.1 to 1
- optimum: float32 [2, 512, 2048], P('scen', 'lx', 'ly'), may hold values from -4 to 4
- observed: float32 [2, 512, 2048], P('scen', 'lx', 'ly'), may hold values from 0 to 1.5
- obs_step: int32 [2, 512], P('scen', 'lx'), may hold values from 1 to 2
- land_code: int32 [512, 2048], P('lx', 'ly'), may hold values 0 or 1
- maps: float32 [2, 512, 2048], P(None, 'lx', 'ly'), may hold values from -4 to 4
- first_moment: float32 [2, 512, 2048], P(None, 'lx', 'ly'), may hold values from -3 to 3
- second_moment: float32 [2, 512, 2048], P(None, 'lx', 'ly'), may hold values from 0.01 to 1
Outputs:
- new_maps: float32 [2, 512, 2048], P(None, 'lx', 'ly')
- new_first: float32 [2, 512, 2048], P(None, 'lx', 'ly')
- new_second: float32 [2, 512, 2048], P(None, 'lx', 'ly')
The draws below stay inside these ranges and needn't reach their ends.
Inputs may be any that keep to these rules, and one draw needn't show every extreme that they name: `land_code`: 1 marks land, 0 sea.
All inputs are finite; a program needn't handle non-finite values. No bound on the sum of `land_code` on one device may be relied on, other than what follows from the above.
Results may differ from the reference program's by a relative error of at most 0.0003.
Values sent between devices are 32-bit elements; how exact they have to be, the bound alone decides.
No kernel may reach another device: no remote copies, remote signals or barrier semaphores. Data moves between devices by JAX's collectives and lax.ppermute only.
A program may use at most 64 MiB of HBM per device.

```python
import math
import jax
import jax.numpy as jnp
from jax import lax

STEPS = 2
ADAM_STEP = 10
SCEN = 2
GX = 512
GY = 2048


def plant(drawn, key, least, top_value):
    shape = drawn.shape
    place = [jax.random.randint(jax.random.fold_in(key, axis), (), 0, shape[axis]) for axis in range(len(shape))]
    drawn = drawn.at[tuple(place)].set(least)
    longest = shape.index(max(shape))
    place[longest] = (place[longest] + 1) % shape[longest]
    return drawn.at[tuple(place)].set(top_value)


def block_levels(rng, extent, cuts, smallest, top_value):
    loudness, own = 1.0, jax.random.fold_in(rng, 6)
    for position, shards_of in cuts:
        heights = jnp.exp(jax.random.uniform(jax.random.fold_in(own, position), (shards_of,), jnp.float32, smallest / len(cuts), top_value / len(cuts)))
        loudness = loudness * jnp.repeat(heights, extent[position] // shards_of).reshape([-1 if axis == position else 1 for axis in range(len(extent))])
    return loudness


def normal_values(stream_key, dims, spread, most, split=(), kind=jnp.bfloat16):
    array = jax.random.normal(stream_key, dims, jnp.float32) * spread
    if len(split) > 0:
        array = block_levels(stream_key, dims, split, -0.22, 0.18) * array
    return jnp.clip(array, min=-most, max=most).astype(kind)


def setup_inputs(seed: int = 0) -> dict:
    key_list = jax.random.split(jax.random.key(seed), 11)
    return {
        "density": jnp.clip(0.2 + 1.3 * jax.random.uniform(key_list[0], (SCEN, GX, GY), jnp.float32) ** block_levels(key_list[0], (SCEN, GX, GY), ((0, 2), (1, 4), (2, 4)), -0.2, 0.2), 0.2, 1.5),
        "trait": normal_values(key_list[1], (SCEN, GX, GY), 1.0, 4.0, ((0, 2), (1, 4), (2, 4)), jnp.float32),
        "variance": jnp.clip(0.1 + 0.9 * jax.random.uniform(key_list[2], (SCEN, GX, GY), jnp.float32) ** block_levels(key_list[2], (SCEN, GX, GY), ((0, 2), (1, 4), (2, 4)), -0.2, 0.2), 0.1, 1.0),
        "optimum": normal_values(key_list[3], (SCEN, GX, GY), 1.0, 4.0, ((0, 2), (1, 4), (2, 4)), jnp.float32),
        "observed": jnp.clip(1.5 * jax.random.uniform(key_list[4], (SCEN, GX, GY), jnp.float32) ** block_levels(key_list[4], (SCEN, GX, GY), ((0, 2), (1, 4), (2, 4)), -0.2, 0.2), 0.0, 1.5),
        "obs_step": plant(jax.random.randint(key_list[5], (SCEN, GX), 1, STEPS + 1), jax.random.fold_in(key_list[5], 1), 1, STEPS).astype(jnp.int32),
        "land_code": plant((jax.random.randint(key_list[6], (GX, GY), 0, 8) < 7).astype(jnp.int32), jax.random.fold_in(key_list[6], 1), 0, 1),
        "maps": normal_values(key_list[7], (2, GX, GY), 1.0, 4.0, ((1, 4), (2, 4)), jnp.float32),
        "first_moment": normal_values(key_list[8], (2, GX, GY), 0.5, 3.0, ((1, 4), (2, 4)), jnp.float32),
        "second_moment": jnp.clip(jnp.exp(math.log(1.0) - 4.6051702 * jax.random.uniform(key_list[9], (2, GX, GY), jnp.float32) ** block_levels(key_list[9], (2, GX, GY), ((1, 4), (2, 4)), -0.2, 0.2)), 0.01, 1.0),
    }


REACH_MAX = 0.2
PRIOR_WEIGHT = 0.1
GROWTH_RATE = 0.5
MUTATION_INPUT = 0.02
LEARN_RATE = 0.01
BETA_FIRST = 0.9
BETA_SECOND = 0.999
ADAM_EPS = 1e-08
LOSS_WEIGHT = 2.0

def interior(values):
    return values[..., 1:-1, 1:-1]

def advance(fields, raw_maps, optimum_map, land_frac):
    density_now, trait_now, variance_now = (fields[0], fields[1], fields[2])
    reach_map = REACH_MAX * jax.nn.sigmoid(raw_maps[0])
    selection = jax.nn.softplus(interior(raw_maps[1]))
    carried = density_now * trait_now
    moment_two = density_now * (variance_now + trait_now * trait_now)
    reach_mid = interior(reach_map)
    land_mid = interior(land_frac)
    cuts = ((slice(2, None), slice(1, -1)), (slice(None, -2), slice(1, -1)), (slice(1, -1), slice(2, None)), (slice(1, -1), slice(None, -2)))
    spread_density = interior(density_now)
    spread_carried = interior(carried)
    spread_moment = interior(moment_two)
    for row_cut, col_cut in cuts:
        weight = 0.5 * (reach_mid + reach_map[row_cut, col_cut]) * land_mid * land_frac[row_cut, col_cut]
        spread_density = spread_density + weight * (density_now[row_cut, col_cut] - interior(density_now))
        spread_carried = spread_carried + weight * (carried[row_cut, col_cut] - interior(carried))
        spread_moment = spread_moment + weight * (moment_two[row_cut, col_cut] - interior(moment_two))
    trait_mid = interior(trait_now)
    variance_mid = interior(variance_now)
    denominator = spread_density + PRIOR_WEIGHT
    trait_spread = (spread_carried + PRIOR_WEIGHT * trait_mid) / denominator
    second_spread = (spread_moment + PRIOR_WEIGHT * (variance_mid + trait_mid * trait_mid)) / denominator
    variance_spread = second_spread - trait_spread * trait_spread
    offset = trait_spread - interior(optimum_map)
    growth = land_mid * (GROWTH_RATE * (1.0 - spread_density) - 0.5 * selection * (offset * offset + variance_spread))
    density_new = spread_density * jnp.exp(growth)
    response = selection * variance_spread
    trait_new = trait_spread - response * offset / (1.0 + response)
    variance_new = variance_spread / (1.0 + response) + MUTATION_INPUT
    return jnp.stack([density_new, trait_new, variance_new])

def adam_update(raw_maps, first_now, second_now, gradient):
    first_new = BETA_FIRST * first_now + (1.0 - BETA_FIRST) * gradient
    second_new = BETA_SECOND * second_now + (1.0 - BETA_SECOND) * gradient * gradient
    first_hat = first_new / (1.0 - BETA_FIRST ** ADAM_STEP)
    second_hat = second_new / (1.0 - BETA_SECOND ** ADAM_STEP)
    maps_new = raw_maps - LEARN_RATE * first_hat / (jnp.sqrt(second_hat) + ADAM_EPS)
    return (maps_new, first_new, second_new)

def pad_cells(values):
    return jnp.pad(values, ((0, 0), (1, 1), (1, 1)))

def scenario_loss(raw_maps, density_s, trait_s, variance_s, optimum_s, observed_s, step_s, land_frac):
    fields = jnp.stack([density_s, trait_s, variance_s])
    loss_total = jnp.float32(0.0)
    for step_index in range(STEPS):
        fields = advance(pad_cells(fields), pad_cells(raw_maps), jnp.pad(optimum_s, 1), jnp.pad(land_frac, 1))
        chosen = (step_s == step_index + 1).astype(jnp.float32)[:, None]
        mismatch = fields[0] - observed_s
        loss_total = loss_total + LOSS_WEIGHT * jnp.sum(chosen * land_frac * mismatch * mismatch)
    return loss_total

def reference(density, trait, variance, optimum, observed, obs_step, land_code, maps, first_moment, second_moment):
    land_frac = land_code.astype(jnp.float32)
    grad_fn = jax.grad(scenario_loss)

    def accumulate(carry_sum, items):
        density_s, trait_s, variance_s, optimum_s, observed_s, step_s = items
        return (carry_sum + grad_fn(maps, density_s, trait_s, variance_s, optimum_s, observed_s, step_s, land_frac), None)
    gradient, _ = lax.scan(accumulate, jnp.zeros(maps.shape, jnp.float32), (density, trait, variance, optimum, observed, obs_step))
    return adam_update(maps, first_moment, second_moment, gradient)
```

```python
import functools

import jax
import jax.numpy as jnp
from jax import lax
from jax.experimental import pallas as pl
from jax.experimental.pallas import tpu as pltpu
from jax.sharding import PartitionSpec as P

STEPS = 2
ADAM_STEP = 10
REACH_MAX = 0.2
PRIOR_WEIGHT = 0.1
GROWTH_RATE = 0.5
MUTATION_INPUT = 0.02
LEARN_RATE = 0.01
BETA_FIRST = 0.9
BETA_SECOND = 0.999
ADAM_EPS = 1e-08
LOSS_WEIGHT = 2.0

F32 = jnp.float32
LANES = 128
EDGE = 8
HALO = 4
DENSITY, TRAIT, VARIANCE, DISPERSAL, SELECTION, OPTIMUM, LAND, OBSERVED = range(8)
FIELDS = 8
VMEM_BYTES = 48 * 1024 * 1024
SAVED = (
    "half",
    "land",
    "select",
    "n0",
    "q0",
    "m0",
    "wd",
    "wr",
    "lr",
    "dr0n",
    "dr0q",
    "dr0m",
    "e",
    "d",
    "vs",
    "p",
    "zs",
    "r",
    "n1",
    "q1",
    "m1",
    "z1",
    "u1",
    "dr1n",
    "dr1q",
    "dr1m",
    "a2n",
    "a2q",
    "a2m",
    "gsel",
    "gd",
    "gr",
    "a1n",
    "a1q",
    "a1m",
)


def reciprocal(value):
    guess = pl.reciprocal(value, approx=True)
    return guess * (2.0 - value * guess)


def sigmoid(value):
    return 0.5 + 0.5 * jnp.tanh(0.5 * value)


def dynamics(slabs, tiles, load, steps_at, keep, put):
    shape = (tiles, 8, LANES)
    lane = lax.broadcasted_iota(jnp.int32, shape, 2)
    at_last, at_first = lane == LANES - 1, lane == 0

    def right(value):
        turned = pltpu.roll(value, LANES - 1, 2)
        beside = jnp.concatenate([turned[1:], turned[:1]], 0) if tiles > 1 else turned
        return jnp.where(at_last, beside, turned)

    def left(value):
        turned = pltpu.roll(value, 1, 2)
        beside = jnp.concatenate([turned[-1:], turned[:-1]], 0) if tiles > 1 else turned
        return jnp.where(at_first, beside, turned)

    def down(name, k):
        if k + 1 < slabs:
            return keep[name][k + 1]
        return pltpu.roll(keep[name][0], 7, 1)

    def wrapped(values):
        return [pltpu.roll(value, 1, 1) for value in values]

    def row_fluxes(names, k):
        weight = keep["wd"][k]
        gaps = [down(name, k) - keep[name][k] for name in names]
        return gaps, [weight * gap for gap in gaps]

    def spread(names, k, above):
        row_gaps, row_flux = row_fluxes(names, k)
        weight = keep["wr"][k]
        out, col_gaps = [], []
        for name, flux, before in zip(names, row_flux, above):
            value = keep[name][k]
            gap = right(value) - value
            col_flux = weight * gap
            out.append(value + (flux - before) + (col_flux - left(col_flux)))
            col_gaps.append(gap)
        return out, row_gaps, col_gaps, row_flux

    for k in range(slabs):
        keep["half"][k] = 0.5 * REACH_MAX * sigmoid(load(DISPERSAL, k))
        keep["land"][k] = load(LAND, k)
        raw = load(SELECTION, k)
        keep["select"][k] = jnp.maximum(raw, 0.0) + jnp.log(1.0 + jnp.exp(-jnp.abs(raw)))
        n, z, v = load(DENSITY, k), load(TRAIT, k), load(VARIANCE, k)
        keep["n0"][k] = n
        keep["q0"][k] = n * z
        keep["m0"][k] = n * (v + z * z)

    for k in range(slabs):
        half, land = keep["half"][k], keep["land"][k]
        keep["wd"][k] = (half + down("half", k)) * (land * down("land", k))
        pair = land * right(land)
        keep["lr"][k] = pair
        keep["wr"][k] = (half + right(half)) * pair

    names = ("n0", "q0", "m0")
    above = wrapped(row_fluxes(names, slabs - 1)[1])
    for k in range(slabs):
        (ns, qs, ms), _, col_gaps, above = spread(names, k, above)
        for name, gap in zip(("dr0n", "dr0q", "dr0m"), col_gaps):
            keep[name][k] = gap
        z, v = load(TRAIT, k), load(VARIANCE, k)
        optimum, select, land = load(OPTIMUM, k), keep["select"][k], keep["land"][k]
        r = reciprocal(ns + PRIOR_WEIGHT)
        zs = (qs + PRIOR_WEIGHT * z) * r
        vs = (ms + PRIOR_WEIGHT * (v + z * z)) * r - zs * zs
        d = zs - optimum
        p = reciprocal(1.0 + select * vs)
        e = jnp.exp(land * (GROWTH_RATE * (1.0 - ns) - 0.5 * select * (d * d + vs)))
        n1 = ns * e
        z1 = optimum + p * d
        u1 = vs * p + MUTATION_INPUT + z1 * z1
        for name, value in zip(
            ("e", "d", "vs", "p", "zs", "r", "n1", "q1", "m1", "z1", "u1"),
            (e, d, vs, p, zs, r, n1, n1 * z1, n1 * u1, z1, u1),
        ):
            keep[name][k] = value

    names = ("n1", "q1", "m1")
    above = wrapped(row_fluxes(names, slabs - 1)[1])
    for k in range(slabs):
        (ns, qs, ms), _, col_gaps, above = spread(names, k, above)
        for name, gap in zip(("dr1n", "dr1q", "dr1m"), col_gaps):
            keep[name][k] = gap
        optimum, select, land = load(OPTIMUM, k), keep["select"][k], keep["land"][k]
        r = reciprocal(ns + PRIOR_WEIGHT)
        zs = (qs + PRIOR_WEIGHT * keep["z1"][k]) * r
        es = (ms + PRIOR_WEIGHT * keep["u1"][k]) * r
        vs = es - zs * zs
        d = zs - optimum
        misfit = d * d + vs
        e = jnp.exp(land * (GROWTH_RATE * (1.0 - ns) - 0.5 * select * misfit))
        n2 = ns * e
        weight = jnp.where(steps_at(k) == 2.0, 2.0 * LOSS_WEIGHT * land, 0.0)
        an = weight * (n2 - load(OBSERVED, k))
        b = 0.5 * an * n2
        av = -b * select
        am = av * r
        aq = -2.0 * optimum * am
        keep["gsel"][k] = -b * misfit
        keep["a2n"][k] = an * e - b - (aq * zs + am * es)
        keep["a2q"][k] = aq
        keep["a2m"][k] = am

    names = ("a2n", "a2q", "a2m")
    above = wrapped(row_fluxes(names, slabs - 1)[1])
    for k in range(slabs):
        (an, aq, am), row_gaps, col_gaps, above = spread(names, k, above)
        fields = ("n1", "q1", "m1")
        keep["gd"][k] = sum((down(f, k) - keep[f][k]) * gap for f, gap in zip(fields, row_gaps))
        keep["gr"][k] = sum(keep[f][k] * gap for f, gap in zip(("dr1n", "dr1q", "dr1m"), col_gaps))
        n1, z1, land, select = keep["n1"][k], keep["z1"][k], keep["land"][k], keep["select"][k]
        e, d, vs, p, zs, r = (keep[name][k] for name in ("e", "d", "vs", "p", "zs", "r"))
        av = PRIOR_WEIGHT * keep["a2m"][k] + am * n1
        az = PRIOR_WEIGHT * keep["a2q"][k] + aq * n1 + 2.0 * z1 * av
        weight = jnp.where(steps_at(k) == 1.0, 2.0 * LOSS_WEIGHT * land, 0.0)
        an = an + aq * z1 + am * keep["u1"][k] + weight * (n1 - load(OBSERVED, k))
        b = 0.5 * an * n1 * land
        at = -(az * d + av * vs) * (p * p)
        gsel = keep["gsel"][k] + at * vs - b * (d * d + vs)
        avs = av * p + select * (at - b)
        azs = az * p - 2.0 * (b * select * d + zs * avs)
        aqs, ams = azs * r, avs * r
        keep["a1n"][k] = an * e - b - (aqs * zs + ams * (vs + zs * zs))
        keep["a1q"][k] = aqs
        keep["a1m"][k] = ams
        put(1, k, gsel * sigmoid(load(SELECTION, k)))

    def row_share(k):
        gaps = [down(name, k) - keep[name][k] for name in ("a1n", "a1q", "a1m")]
        fields = [down(name, k) - keep[name][k] for name in ("n0", "q0", "m0")]
        total = keep["gd"][k] + sum(gap * field for gap, field in zip(gaps, fields))
        return total * (keep["land"][k] * down("land", k))

    (above,) = wrapped([row_share(slabs - 1)])
    for k in range(slabs):
        here = row_share(k)
        total = keep["gr"][k]
        for name, field in zip(("a1n", "a1q", "a1m"), ("dr0n", "dr0q", "dr0m")):
            value = keep[name][k]
            total = total + (right(value) - value) * keep[field][k]
        total = total * keep["lr"][k]
        half = keep["half"][k]
        put(0, k, half * (10.0 * half - 1.0) * (here + above + total + left(total)))
        above = here


def step_rows(line):
    return jnp.transpose(jnp.concatenate([line] * (LANES // 8), 0))


def interior_kernel(first, rows, out_first, out_rows, tiles, *refs):
    sources, step_ref, out_ref = refs[:7], refs[7], refs[8]
    fields, codes, step_tile, grads, kept, sems = refs[9:15]
    slabs = rows // 8
    copies = []

    def bring(field, source, target):
        group = [
            pltpu.make_async_copy(
                source.at[pl.ds(first, rows), pl.ds(t * LANES, LANES)], target.at[t], sems.at[field, t]
            )
            for t in range(tiles)
        ]
        for copy in group:
            copy.start()
        copies.extend(group)

    density, trait, variance, optimum, observed, land_code, maps = sources
    bring(DISPERSAL, maps.at[0], fields.at[DISPERSAL])
    bring(LAND, land_code, codes)
    bring(SELECTION, maps.at[1], fields.at[SELECTION])
    bring(DENSITY, density.at[0], fields.at[DENSITY])
    bring(TRAIT, trait.at[0], fields.at[TRAIT])
    bring(VARIANCE, variance.at[0], fields.at[VARIANCE])
    bring(OPTIMUM, optimum.at[0], fields.at[OPTIMUM])
    bring(OBSERVED, observed.at[0], fields.at[OBSERVED])
    line = jnp.broadcast_to(step_ref[0:1, :].astype(F32), (8, LANES))
    step_tile[...] = step_rows(line)
    for copy in copies:
        copy.wait()

    def load(field, k):
        source = codes if field == LAND else fields.at[field]
        parts = [source[t, pl.ds(k, 8, stride=slabs), :] for t in range(tiles)]
        return jnp.stack(parts).astype(F32)

    def steps_at(k):
        part = step_tile[pl.ds(first + k, 8, stride=slabs), :]
        return jnp.broadcast_to(part[None], (tiles, 8, LANES))

    def put(which, k, value):
        for t in range(tiles):
            grads[which, t, pl.ds(k, 8, stride=slabs), :] = value[t]

    keep = {name: kept.at[index] for index, name in enumerate(SAVED)}
    dynamics(slabs, tiles, load, steps_at, keep, put)
    skip = out_first - first
    for which in range(2):
        for t in range(tiles):
            out_ref[which, :, t * LANES : (t + 1) * LANES] = grads[which, t, skip : skip + out_rows, :]


def interior(first, rows, out_first, out_rows, sources, steps):
    columns = sources[0].shape[-1]
    tiles = columns // LANES
    kernel = functools.partial(interior_kernel, first, rows, out_first, out_rows, tiles)
    return pl.pallas_call(
        kernel,
        out_shape=jax.ShapeDtypeStruct((2, out_rows, columns), F32),
        in_specs=[pl.BlockSpec(memory_space=pl.ANY)] * 7 + [pl.BlockSpec(memory_space=pltpu.VMEM)],
        out_specs=pl.BlockSpec(memory_space=pltpu.VMEM),
        scratch_shapes=[
            pltpu.VMEM((FIELDS, tiles, rows, LANES), F32),
            pltpu.VMEM((tiles, rows, LANES), jnp.int32),
            pltpu.VMEM((LANES, LANES), F32),
            pltpu.VMEM((2, tiles, rows, LANES), F32),
            pltpu.VMEM((len(SAVED), rows // 8, tiles, 8, LANES), F32),
            pltpu.SemaphoreType.DMA((FIELDS, tiles)),
        ],
        compiler_params=pltpu.CompilerParams(vmem_limit_bytes=VMEM_BYTES),
        name=f"interior_{out_first}",
    )(*sources, steps)


def field_blocks(refs):
    density, trait, variance, optimum, observed, land_code, maps = refs
    return [
        density[0],
        trait[0],
        variance[0],
        maps[0],
        maps[1],
        optimum[0],
        land_code[...].astype(F32),
        observed[0],
    ]


def columns_kernel(*refs):
    firsts, lasts, left_ref, right_ref = refs[:7], refs[7:14], refs[14], refs[15]
    rows = left_ref.shape[-1]
    lane = lax.broadcasted_iota(jnp.int32, (rows, LANES), 1)
    packed = jnp.zeros((rows, LANES), F32)
    for field, (first, last) in enumerate(zip(field_blocks(firsts), field_blocks(lasts))):
        both = jnp.where(lane < EDGE, first, last)
        turned = pltpu.roll(both, 16 * field, 1) if field else both
        place = (lane - 16 * field + EDGE) % LANES
        packed = jnp.where(place < 2 * EDGE, turned, packed)
    flipped = jnp.transpose(packed)
    for field in range(FIELDS):
        left_ref[field] = flipped[16 * field : 16 * field + EDGE]
        start = (16 * field - EDGE) % LANES
        right_ref[field] = flipped[start : start + EDGE]


def block_specs(sources, rows, columns, at):
    specs = []
    for source in sources:
        if source.ndim == 2:
            specs.append(pl.BlockSpec((rows, columns), lambda i, at=at: at))
        else:
            specs.append(pl.BlockSpec((source.shape[0], rows, columns), lambda i, at=at: (0, *at)))
    return specs


def whole_spec(array):
    return pl.BlockSpec(array.shape, lambda i: (0,) * array.ndim)


def pack_columns(sources):
    rows, columns = sources[0].shape[1:]
    specs = block_specs(sources, rows, LANES, (0, 0))
    specs += block_specs(sources, rows, LANES, (0, columns // LANES - 1))
    shape = jax.ShapeDtypeStruct((FIELDS, EDGE, rows), F32)
    return pl.pallas_call(
        columns_kernel,
        grid=(1,),
        out_shape=[shape, shape],
        in_specs=specs,
        out_specs=[whole_spec(shape)] * 2,
        compiler_params=pltpu.CompilerParams(vmem_limit_bytes=VMEM_BYTES),
        name="pack_columns",
    )(*sources, *sources)


def rows_kernel(tiles, *refs):
    tops, bottoms = refs[:7], refs[7:14]
    own_left, own_right, from_left, from_right, step_ref, up_ref, down_ref = refs[14:]
    sub = lax.broadcasted_iota(jnp.int32, (8, tiles * LANES), 0)
    top, bottom = field_blocks(tops), field_blocks(bottoms)
    for pair in range(FIELDS // 2):
        upward = jnp.where(sub < HALO, top[2 * pair], pltpu.roll(top[2 * pair + 1], HALO, 0))
        downward = jnp.where(sub < HALO, pltpu.roll(bottom[2 * pair + 1], HALO, 0), bottom[2 * pair])
        for t in range(tiles):
            up_ref[pair * tiles + t] = upward[:, t * LANES : (t + 1) * LANES]
            down_ref[pair * tiles + t] = downward[:, t * LANES : (t + 1) * LANES]
    lane = lax.broadcasted_iota(jnp.int32, (8, LANES), 1)
    base = FIELDS // 2 * tiles
    for index, strip in enumerate((from_left, own_left, own_right, from_right)):
        packed = jnp.zeros((8, LANES), F32)
        for field in range(FIELDS):
            turned = pltpu.roll(strip[field], 8 * field, 1) if field else strip[field]
            place = (lane - 8 * field + HALO) % LANES
            packed = jnp.where(place < 2 * HALO, turned, packed)
        up_ref[base + index] = packed
        down_ref[base + index] = packed
    line = jnp.broadcast_to(step_ref[0:1, :].astype(F32), (8, LANES))
    up_ref[base + 4] = line
    down_ref[base + 4] = line


def pack_rows(sources, strips, steps):
    rows, columns = sources[0].shape[1:]
    tiles = columns // LANES
    specs = block_specs(sources, EDGE, columns, (0, 0))
    specs += block_specs(sources, EDGE, columns, (rows // EDGE - 1, 0))
    specs += [whole_spec(strip) for strip in strips] + [whole_spec(steps)]
    shape = jax.ShapeDtypeStruct((FIELDS // 2 * tiles + 5, 8, LANES), F32)
    return pl.pallas_call(
        functools.partial(rows_kernel, tiles),
        grid=(1,),
        out_shape=[shape, shape],
        in_specs=specs,
        out_specs=[whole_spec(shape)] * 2,
        compiler_params=pltpu.CompilerParams(vmem_limit_bytes=VMEM_BYTES),
        name="pack_rows",
    )(*sources, *sources, *strips, steps)


def edges_kernel(tiles, place_ref, *refs):
    tops, bottoms = refs[:7], refs[7:14]
    own_left, own_right, from_left, from_right, step_ref, from_above, from_below, out_ref = refs[14:22]
    row_strip, col_strip, row_step, row_grad, col_grad, row_keep, col_keep = refs[22:]
    base = FIELDS // 2 * tiles
    has_above, has_below, has_left, has_right = (place_ref[i] for i in range(4))
    top, bottom = field_blocks(tops), field_blocks(bottoms)
    lane = lax.broadcasted_iota(jnp.int32, (8, LANES), 1)
    sub = lax.broadcasted_iota(jnp.int32, (8, LANES), 0)

    corners = [
        jnp.where((lane % 8) < HALO, from_below[base + index], from_above[base + index]) for index in range(4)
    ]
    beside = [[None] * 4 for _ in range(FIELDS)]
    for field in range(FIELDS):
        for index, strip in enumerate((from_left, own_left, own_right, from_right)):
            value = strip[field]
            outer = pltpu.roll(corners[index], (LANES - 8 * field) % LANES, 1) if field else corners[index]
            if field == LAND:
                outer = outer * jnp.where(lane < LANES // 2, has_below, has_above)
                if index == 0:
                    value, outer = value * has_left, outer * has_left
                if index == 3:
                    value, outer = value * has_right, outer * has_right
            col_strip[field, 0, 8 * index : 8 * index + 8, :] = value
            col_strip[field, 1, 8 * index : 8 * index + 8, :] = outer
            beside[field][index] = (value, outer)

    def lined(value, outer):
        out = jnp.where(lane < 8, pltpu.roll(outer, 8, 1), pltpu.roll(value, 8, 1))
        out = jnp.where(lane < 16, out, pltpu.roll(value, 24, 1))
        return jnp.where(lane < 24, out, pltpu.roll(outer, 24, 1))

    zeros = jnp.zeros((8, LANES), F32)
    stack = []
    for index in range(LANES // 8):
        here = lined(*beside[index][3]) if index < FIELDS else zeros
        following = (index + 1) % (LANES // 8)
        after = lined(*beside[following][0]) if following < FIELDS else zeros
        stack.append(jnp.where(sub < HALO, here, after))
    flipped = jnp.transpose(jnp.concatenate(stack, 0))[:32]
    own_step = jnp.broadcast_to(step_ref[0:1, :].astype(F32), (8, LANES))
    outer_step = jnp.where(lane < LANES // 2, from_below[base + 4], from_above[base + 4])
    row_step[...] = step_rows(lined(own_step, outer_step))[:32]
    for field in range(FIELDS):
        for t in range(tiles):
            above, below = from_above[field // 2 * tiles + t], from_below[field // 2 * tiles + t]
            if field % 2:
                above, below = pltpu.roll(above, HALO, 0), pltpu.roll(below, HALO, 0)
            if field == LAND:
                above, below = above * has_above, below * has_below
            own = slice(t * LANES, (t + 1) * LANES)
            for index, value in enumerate((above, top[field][:, own], bottom[field][:, own], below)):
                row_strip[field, t, 8 * index : 8 * index + 8, :] = value
        row_strip[field, tiles] = pltpu.roll(flipped, (LANES - 8 * field) % LANES, 1) if field else flipped

    slabs = 3
    for strip, grad, kept, count in (
        (row_strip, row_grad, row_keep, tiles + 1),
        (col_strip, col_grad, col_keep, 2),
    ):
        on_rows = strip is row_strip

        def load(field, k):
            parts = [strip[field, t, pl.ds(HALO + k, 8, stride=slabs), :] for t in range(count)]
            return jnp.stack(parts)

        def steps_at(k):
            if on_rows:
                part = row_step[pl.ds(HALO + k, 8, stride=slabs), :]
                return jnp.broadcast_to(part[None], (count, 8, LANES))
            return jnp.stack([own_step, outer_step])

        def put(which, k, value):
            for t in range(count):
                grad[which, t, pl.ds(HALO + k, 8, stride=slabs), :] = value[t]

        keep = {name: kept.at[index] for index, name in enumerate(SAVED)}
        dynamics(slabs, count, load, steps_at, keep, put)
    for which in range(2):
        for t in range(tiles):
            out_ref[which, :, t * LANES : (t + 1) * LANES] = jnp.where(
                sub < HALO, row_grad[which, t, 8:16, :], row_grad[which, t, 16:24, :]
            )
        out_ref[which, :, tiles * LANES :] = jnp.where(
            sub < HALO, col_grad[which, 0, 8:16, :], col_grad[which, 0, 16:24, :]
        )


def edges(place, sources, strips, steps, from_above, from_below):
    rows, columns = sources[0].shape[1:]
    tiles = columns // LANES
    specs = [pl.BlockSpec(memory_space=pltpu.SMEM)]
    specs += block_specs(sources, EDGE, columns, (0, 0))
    specs += block_specs(sources, EDGE, columns, (rows // EDGE - 1, 0))
    rest = [*strips, steps, from_above, from_below]
    specs += [whole_spec(array) for array in rest]
    shape = jax.ShapeDtypeStruct((2, EDGE, columns + LANES), F32)
    return pl.pallas_call(
        functools.partial(edges_kernel, tiles),
        grid=(1,),
        out_shape=shape,
        in_specs=specs,
        out_specs=whole_spec(shape),
        scratch_shapes=[
            pltpu.VMEM((FIELDS, tiles + 1, 32, LANES), F32),
            pltpu.VMEM((FIELDS, 2, 32, LANES), F32),
            pltpu.VMEM((32, LANES), F32),
            pltpu.VMEM((2, tiles + 1, 32, LANES), F32),
            pltpu.VMEM((2, 2, 32, LANES), F32),
            pltpu.VMEM((len(SAVED), 3, tiles + 1, 8, LANES), F32),
            pltpu.VMEM((len(SAVED), 3, 2, 8, LANES), F32),
        ],
        compiler_params=pltpu.CompilerParams(vmem_limit_bytes=VMEM_BYTES),
        name="edges",
    )(place, *sources, *sources, *rest)


def update_kernel(parts, terms, maps_ref, first_ref, second_ref, *refs):
    grads, edge_refs = refs[: parts * terms], refs[parts * terms : (parts + 1) * terms]
    new_maps, new_first, new_second = refs[(parts + 1) * terms :]
    rows, columns = maps_ref.shape[1:]
    tiles = columns // LANES
    lane = lax.broadcasted_iota(jnp.int32, (rows, LANES), 1)
    sub = lax.broadcasted_iota(jnp.int32, (EDGE, LANES), 0)
    edge = sum(ref[...] for ref in edge_refs)
    strips = [edge[which, :, columns:] for which in range(2)]
    blank = jnp.zeros((LANES - 2 * EDGE, LANES), F32)
    flipped = jnp.transpose(jnp.concatenate([*strips, blank], 0))
    height = rows // parts
    for which in range(2):
        for t in range(tiles):
            own = slice(t * LANES, (t + 1) * LANES)
            grad = jnp.concatenate(
                [sum(ref[which, :, own] for ref in grads[part * terms : (part + 1) * terms]) for part in range(parts)],
                0,
            )
            outer = edge[which, :, own]
            grad = jnp.concatenate(
                [
                    jnp.where(sub < HALO, outer, grad[:EDGE]),
                    grad[EDGE:-EDGE],
                    jnp.where(sub < HALO, grad[-EDGE:], outer),
                ],
                0,
            )
            if t == 0:
                beside = pltpu.roll(flipped, LANES - EDGE * which, 1) if which else flipped
                grad = jnp.where(lane < HALO, beside, grad)
            if t == tiles - 1:
                beside = pltpu.roll(flipped, LANES - EDGE * (which + 1), 1)
                grad = jnp.where(lane >= LANES - HALO, beside, grad)
            first = BETA_FIRST * first_ref[which, :, own] + (1.0 - BETA_FIRST) * grad
            second = BETA_SECOND * second_ref[which, :, own] + (1.0 - BETA_SECOND) * grad * grad
            new_first[which, :, own] = first
            new_second[which, :, own] = second
            scale = jnp.sqrt(second * (1.0 / (1.0 - BETA_SECOND**ADAM_STEP))) + ADAM_EPS
            change = (LEARN_RATE / (1.0 - BETA_FIRST**ADAM_STEP)) * first
            new_maps[which, :, own] = maps_ref[which, :, own] - change * reciprocal(scale)


def update(maps, first_moment, second_moment, grads, edge_grads):
    parts, terms = len(grads), len(edge_grads)
    flat = [term for grad in grads for term in grad]
    shape = jax.ShapeDtypeStruct(maps.shape, F32)
    operands = [maps, first_moment, second_moment, *flat, *edge_grads]
    return pl.pallas_call(
        functools.partial(update_kernel, parts, terms),
        out_shape=[shape] * 3,
        in_specs=[pl.BlockSpec(memory_space=pltpu.VMEM)] * len(operands),
        out_specs=[pl.BlockSpec(memory_space=pltpu.VMEM)] * 3,
        compiler_params=pltpu.CompilerParams(vmem_limit_bytes=VMEM_BYTES),
        name="update",
    )(*operands)


def shifts(axis):
    count = lax.axis_size(axis)
    forward = [(i, (i + 1) % count) for i in range(count)]
    return forward, [(target, source) for source, target in forward]


def both_scenarios(value):
    count = lax.axis_size("scen")
    if count == 2:
        return [value, lax.ppermute(value, "scen", [(0, 1), (1, 0)])]
    return [lax.psum(value, "scen")]


def shards(
    density,
    trait,
    variance,
    optimum,
    observed,
    obs_step,
    land_code,
    maps,
    first_moment,
    second_moment,
):
    sources = (density, trait, variance, optimum, observed, land_code, maps)
    rows = maps.shape[1]
    middle = rows // 2
    upper = interior(0, middle + EDGE, 0, middle, sources, obs_step)
    upper_terms = both_scenarios(upper)
    own_left, own_right = pack_columns(sources)
    rightward, leftward = shifts("ly")
    from_left = lax.ppermute(own_right, "ly", rightward)
    from_right = lax.ppermute(own_left, "ly", leftward)
    lower = interior(middle - EDGE, middle + EDGE, middle, middle, sources, obs_step)
    lower_terms = both_scenarios(lower)
    strips = (own_left, own_right, from_left, from_right)
    up, down = pack_rows(sources, strips, obs_step)
    downward, upward = shifts("lx")
    from_above = lax.ppermute(down, "lx", downward)
    from_below = lax.ppermute(up, "lx", upward)
    row, column = lax.axis_index("lx"), lax.axis_index("ly")
    place = jnp.stack(
        [row > 0, row < lax.axis_size("lx") - 1, column > 0, column < lax.axis_size("ly") - 1]
    ).astype(F32)
    outer = edges(place, sources, strips, obs_step, from_above, from_below)
    outer_terms = both_scenarios(outer)
    return tuple(update(maps, first_moment, second_moment, [upper_terms, lower_terms], outer_terms))


def solution(mesh):
    in_specs = (
        P("scen", "lx", "ly"),
        P("scen", "lx", "ly"),
        P("scen", "lx", "ly"),
        P("scen", "lx", "ly"),
        P("scen", "lx", "ly"),
        P("scen", "lx"),
        P("lx", "ly"),
        P(None, "lx", "ly"),
        P(None, "lx", "ly"),
        P(None, "lx", "ly"),
    )
    out_specs = (P(None, "lx", "ly"), P(None, "lx", "ly"), P(None, "lx", "ly"))
    return jax.shard_map(shards, mesh=mesh, in_specs=in_specs, out_specs=out_specs, check_vma=False)
```

```python
import functools

import jax
import jax.numpy as jnp
from jax import lax
from jax.experimental import pallas as pl
from jax.experimental.pallas import tpu as pltpu
from jax.sharding import PartitionSpec as P

STEPS = 2
ADAM_STEP = 10
REACH_MAX = 0.2
PRIOR_WEIGHT = 0.1
GROWTH_RATE = 0.5
MUTATION_INPUT = 0.02
LEARN_RATE = 0.01
BETA_FIRST = 0.9
BETA_SECOND = 0.999
ADAM_EPS = 1e-08
LOSS_WEIGHT = 2.0

F32 = jnp.float32
LANES = 128
EDGE = 8
HALO = 4
DENSITY, TRAIT, VARIANCE, DISPERSAL, SELECTION, OPTIMUM, LAND, OBSERVED = range(8)
FIELDS = 8
GROUP = 3
WINDOW_US, EDGES_US = 4, 20
VMEM_BYTES = 16 * 1024 * 1024
SAVED = (
    "half",
    "land",
    "select",
    "n0",
    "q0",
    "m0",
    "wd",
    "wr",
    "lr",
    "dr0n",
    "dr0q",
    "dr0m",
    "e",
    "d",
    "vs",
    "p",
    "zs",
    "r",
    "n1",
    "q1",
    "m1",
    "z1",
    "u1",
    "dr1n",
    "dr1q",
    "dr1m",
    "a2n",
    "a2q",
    "a2m",
    "gsel",
    "gd",
    "gr",
    "a1n",
    "a1q",
    "a1m",
)


def cost(microseconds):
    return pl.CostEstimate(flops=int(microseconds * 1e9), transcendentals=0, bytes_accessed=int(microseconds * 3.6e6))


def reciprocal(value):
    guess = pl.reciprocal(value, approx=True)
    return guess * (2.0 - value * guess)


def sigmoid(value):
    return 0.5 + 0.5 * jnp.tanh(0.5 * value)


def dynamics(slabs, group, tiles, load, steps_at, keep, put):
    shape = (tiles, 8, LANES)
    lane = lax.broadcasted_iota(jnp.int32, shape, 2)
    at_last, at_first = lane == LANES - 1, lane == 0

    def right(value):
        turned = pltpu.roll(value, LANES - 1, 2)
        beside = jnp.concatenate([turned[1:], turned[:1]], 0) if tiles > 1 else turned
        return jnp.where(at_last, beside, turned)

    def left(value):
        turned = pltpu.roll(value, 1, 2)
        beside = jnp.concatenate([turned[-1:], turned[:-1]], 0) if tiles > 1 else turned
        return jnp.where(at_first, beside, turned)

    def each_slab(body, carry=()):
        def step(index, carry):
            for offset in range(group):
                carry = body(index * group + offset, carry)
            return carry

        if group == slabs:
            return step(0, carry)
        return lax.fori_loop(0, slabs // group, step, carry)

    def close(names):
        for name in names:
            keep[name][slabs] = pltpu.roll(keep[name][0], 7, 1)

    def wrapped(values):
        return tuple(pltpu.roll(value, 1, 1) for value in values)

    def down_gap(name, k):
        return keep[name][k + 1] - keep[name][k]

    def row_fluxes(names, k):
        weight = keep["wd"][k]
        gaps = [down_gap(name, k) for name in names]
        return gaps, tuple(weight * gap for gap in gaps)

    def spread(names, k, above):
        row_gaps, row_flux = row_fluxes(names, k)
        weight = keep["wr"][k]
        out, col_gaps = [], []
        for name, flux, before in zip(names, row_flux, above):
            value = keep[name][k]
            gap = right(value) - value
            col_flux = weight * gap
            out.append(value + (flux - before) + (col_flux - left(col_flux)))
            col_gaps.append(gap)
        return out, row_gaps, col_gaps, row_flux

    def begin(k, _):
        keep["half"][k] = 0.5 * REACH_MAX * sigmoid(load(DISPERSAL, k))
        keep["land"][k] = load(LAND, k)
        raw = load(SELECTION, k)
        keep["select"][k] = jnp.maximum(raw, 0.0) + jnp.log(1.0 + jnp.exp(-jnp.abs(raw)))
        n, z, v = load(DENSITY, k), load(TRAIT, k), load(VARIANCE, k)
        keep["n0"][k] = n
        keep["q0"][k] = n * z
        keep["m0"][k] = n * (v + z * z)
        return ()

    each_slab(begin)
    close(("half", "land", "n0", "q0", "m0"))

    def weigh(k, _):
        half, land = keep["half"][k], keep["land"][k]
        keep["wd"][k] = (half + keep["half"][k + 1]) * (land * keep["land"][k + 1])
        pair = land * right(land)
        keep["lr"][k] = pair
        keep["wr"][k] = (half + right(half)) * pair
        return ()

    each_slab(weigh)
    first_names, second_names = ("n0", "q0", "m0"), ("n1", "q1", "m1")

    def first_step(k, above):
        (ns, qs, ms), _, col_gaps, above = spread(first_names, k, above)
        for name, gap in zip(("dr0n", "dr0q", "dr0m"), col_gaps):
            keep[name][k] = gap
        z, v = load(TRAIT, k), load(VARIANCE, k)
        optimum, select, land = load(OPTIMUM, k), keep["select"][k], keep["land"][k]
        r = reciprocal(ns + PRIOR_WEIGHT)
        zs = (qs + PRIOR_WEIGHT * z) * r
        vs = (ms + PRIOR_WEIGHT * (v + z * z)) * r - zs * zs
        d = zs - optimum
        p = reciprocal(1.0 + select * vs)
        e = jnp.exp(land * (GROWTH_RATE * (1.0 - ns) - 0.5 * select * (d * d + vs)))
        n1 = ns * e
        z1 = optimum + p * d
        u1 = vs * p + MUTATION_INPUT + z1 * z1
        for name, value in zip(
            ("e", "d", "vs", "p", "zs", "r", "n1", "q1", "m1", "z1", "u1"),
            (e, d, vs, p, zs, r, n1, n1 * z1, n1 * u1, z1, u1),
        ):
            keep[name][k] = value
        return above

    each_slab(first_step, wrapped(row_fluxes(first_names, slabs - 1)[1]))
    close(second_names)

    def second_step(k, above):
        (ns, qs, ms), _, col_gaps, above = spread(second_names, k, above)
        for name, gap in zip(("dr1n", "dr1q", "dr1m"), col_gaps):
            keep[name][k] = gap
        optimum, select, land = load(OPTIMUM, k), keep["select"][k], keep["land"][k]
        r = reciprocal(ns + PRIOR_WEIGHT)
        zs = (qs + PRIOR_WEIGHT * keep["z1"][k]) * r
        es = (ms + PRIOR_WEIGHT * keep["u1"][k]) * r
        vs = es - zs * zs
        d = zs - optimum
        misfit = d * d + vs
        e = jnp.exp(land * (GROWTH_RATE * (1.0 - ns) - 0.5 * select * misfit))
        n2 = ns * e
        weight = jnp.where(steps_at(k) == 2.0, 2.0 * LOSS_WEIGHT * land, 0.0)
        an = weight * (n2 - load(OBSERVED, k))
        b = 0.5 * an * n2
        av = -b * select
        am = av * r
        aq = -2.0 * optimum * am
        keep["gsel"][k] = -b * misfit
        keep["a2n"][k] = an * e - b - (aq * zs + am * es)
        keep["a2q"][k] = aq
        keep["a2m"][k] = am
        return above

    each_slab(second_step, wrapped(row_fluxes(second_names, slabs - 1)[1]))
    second_back, first_back = ("a2n", "a2q", "a2m"), ("a1n", "a1q", "a1m")
    close(second_back)

    def back(k, above):
        (an, aq, am), row_gaps, col_gaps, above = spread(second_back, k, above)
        n_gap, q_gap, m_gap = [down_gap(name, k) * gap for name, gap in zip(second_names, row_gaps)]
        keep["gd"][k] = n_gap + q_gap + m_gap
        n_gap, q_gap, m_gap = [keep[f][k] * gap for f, gap in zip(("dr1n", "dr1q", "dr1m"), col_gaps)]
        keep["gr"][k] = n_gap + q_gap + m_gap
        n1, z1, land, select = keep["n1"][k], keep["z1"][k], keep["land"][k], keep["select"][k]
        e, d, vs, p, zs, r = (keep[name][k] for name in ("e", "d", "vs", "p", "zs", "r"))
        av = PRIOR_WEIGHT * keep["a2m"][k] + am * n1
        az = PRIOR_WEIGHT * keep["a2q"][k] + aq * n1 + 2.0 * z1 * av
        weight = jnp.where(steps_at(k) == 1.0, 2.0 * LOSS_WEIGHT * land, 0.0)
        an = an + aq * z1 + am * keep["u1"][k] + weight * (n1 - load(OBSERVED, k))
        b = 0.5 * an * n1 * land
        at = -(az * d + av * vs) * (p * p)
        gsel = keep["gsel"][k] + at * vs - b * (d * d + vs)
        avs = av * p + select * (at - b)
        azs = az * p - 2.0 * (b * select * d + zs * avs)
        aqs, ams = azs * r, avs * r
        keep["a1n"][k] = an * e - b - (aqs * zs + ams * (vs + zs * zs))
        keep["a1q"][k] = aqs
        keep["a1m"][k] = ams
        put(1, k, gsel * sigmoid(load(SELECTION, k)))
        return above

    each_slab(back, wrapped(row_fluxes(second_back, slabs - 1)[1]))
    close(first_back)

    def row_share(k):
        n_gap, q_gap, m_gap = [down_gap(a, k) * down_gap(f, k) for a, f in zip(first_back, first_names)]
        return (keep["gd"][k] + n_gap + q_gap + m_gap) * (keep["land"][k] * keep["land"][k + 1])

    def finish(k, above):
        here = row_share(k)
        total = keep["gr"][k]
        for name, field in zip(first_back, ("dr0n", "dr0q", "dr0m")):
            value = keep[name][k]
            total = total + (right(value) - value) * keep[field][k]
        total = total * keep["lr"][k]
        half = keep["half"][k]
        put(0, k, half * (10.0 * half - 1.0) * (here + above[0] + total + left(total)))
        return (here,)

    each_slab(finish, wrapped((row_share(slabs - 1),)))


def step_rows(line):
    return jnp.transpose(jnp.concatenate([line] * (LANES // 8), 0))


def fill_kernel(tiles, sources, step_ref, fields, steps, codes, sems):
    density, trait, variance, optimum, observed, land_code, maps = sources
    copies = []
    for field, (source, target) in enumerate(
        (
            (density.at[0], fields.at[DENSITY]),
            (trait.at[0], fields.at[TRAIT]),
            (variance.at[0], fields.at[VARIANCE]),
            (maps.at[0], fields.at[DISPERSAL]),
            (maps.at[1], fields.at[SELECTION]),
            (optimum.at[0], fields.at[OPTIMUM]),
            (land_code, codes),
            (observed.at[0], fields.at[OBSERVED]),
        )
    ):
        for t in range(tiles):
            copies.append(
                pltpu.make_async_copy(source.at[:, pl.ds(t * LANES, LANES)], target.at[t], sems.at[field, t])
            )
    for copy in copies:
        copy.start()
    line = jnp.broadcast_to(step_ref[0:1, :].astype(F32), (8, LANES))
    steps[0] = step_rows(line)
    steps[1] = jnp.broadcast_to(line[0:1], (LANES, LANES))
    for copy in copies:
        copy.wait()
    fields[LAND] = codes[...].astype(F32)


def window_kernel(first, rows, skip, fields, steps, *refs):
    out_ref, grads, kept = refs[-3:]
    tiles = fields.shape[1]
    out_rows = out_ref.shape[1]
    slabs = rows // 8

    def load(field, k):
        return jnp.stack([fields[field, t, pl.ds(first + k, 8, stride=slabs), :] for t in range(tiles)])

    def steps_at(k):
        part = steps[0, pl.ds(first + k, 8, stride=slabs), :]
        return jnp.broadcast_to(part[None], (tiles, 8, LANES))

    def put(which, k, value):
        for t in range(tiles):
            grads[which, t, pl.ds(k, 8, stride=slabs), :] = value[t]

    keep = {name: kept.at[index] for index, name in enumerate(SAVED)}
    dynamics(slabs, GROUP, tiles, load, steps_at, keep, put)
    for which in range(2):
        for t in range(tiles):
            out_ref[which, :, t * LANES : (t + 1) * LANES] = grads[which, t, skip : skip + out_rows, :]


def load_kernel(tiles, *refs):
    sources, step_ref, fields, steps, left_ref, right_ref, codes, sems = refs[:7], *refs[7:]
    fill_kernel(tiles, sources, step_ref, fields, steps, codes, sems)
    columns_kernel(fields, left_ref, right_ref)


def load_tile(sources, obs_step):
    height, columns = sources[0].shape[1:]
    tiles = columns // LANES
    strip = jax.ShapeDtypeStruct((FIELDS, EDGE, height), F32)
    return pl.pallas_call(
        functools.partial(load_kernel, tiles),
        out_shape=[
            jax.ShapeDtypeStruct((FIELDS, tiles, height, LANES), F32),
            jax.ShapeDtypeStruct((2, LANES, LANES), F32),
            strip,
            strip,
        ],
        in_specs=[pl.BlockSpec(memory_space=pltpu.HBM)] * 7 + [pl.BlockSpec(memory_space=pltpu.VMEM)],
        out_specs=[pl.BlockSpec(memory_space=pltpu.VMEM)] * 4,
        scratch_shapes=[
            pltpu.VMEM((tiles, height, LANES), jnp.int32),
            pltpu.SemaphoreType.DMA((FIELDS, tiles)),
        ],
        compiler_params=pltpu.CompilerParams(vmem_limit_bytes=VMEM_BYTES),
        name="load_tile",
    )(*(pltpu.with_memory_space_constraint(source, pltpu.HBM) for source in sources), obs_step)


def window(first, rows, out_first, out_rows, fields, steps, *after):
    tiles = fields.shape[1]
    return pl.pallas_call(
        functools.partial(window_kernel, first, rows, out_first - first),
        out_shape=jax.ShapeDtypeStruct((2, out_rows, tiles * LANES), F32),
        in_specs=[pl.BlockSpec(memory_space=pltpu.VMEM)] * 2 + [pl.BlockSpec(memory_space=pltpu.VMEM)] * len(after),
        out_specs=pl.BlockSpec(memory_space=pltpu.VMEM),
        scratch_shapes=[
            pltpu.VMEM((2, tiles, rows, LANES), F32),
            pltpu.VMEM((len(SAVED), rows // 8 + 1, tiles, 8, LANES), F32),
        ],
        cost_estimate=cost(WINDOW_US),
        compiler_params=pltpu.CompilerParams(vmem_limit_bytes=VMEM_BYTES),
        name=f"window_{out_first}",
    )(fields, steps, *after)


def columns_kernel(fields, left_ref, right_ref):
    tiles, rows = fields.shape[1:3]
    lane = lax.broadcasted_iota(jnp.int32, (rows, LANES), 1)
    packed = jnp.zeros((rows, LANES), F32)
    for field in range(FIELDS):
        both = jnp.where(lane < EDGE, fields[field, 0], fields[field, tiles - 1])
        turned = pltpu.roll(both, 16 * field, 1) if field else both
        place = (lane - 16 * field + EDGE) % LANES
        packed = jnp.where(place < 2 * EDGE, turned, packed)
    flipped = jnp.transpose(packed)
    for field in range(FIELDS):
        left_ref[field] = flipped[16 * field : 16 * field + EDGE]
        start = (16 * field - EDGE) % LANES
        right_ref[field] = flipped[start : start + EDGE]


def in_vmem(kernel, name, out_shape, scratch=()):
    def call(*operands):
        many = isinstance(out_shape, (list, tuple))
        space = pl.BlockSpec(memory_space=pltpu.VMEM)
        return pl.pallas_call(
            kernel,
            out_shape=out_shape,
            in_specs=[space] * len(operands),
            out_specs=[space] * len(out_shape) if many else space,
            scratch_shapes=list(scratch),
            compiler_params=pltpu.CompilerParams(vmem_limit_bytes=VMEM_BYTES),
            name=name,
        )(*operands)

    return call


def rows_kernel(fields, steps, own_left, own_right, from_left, from_right, up_ref, down_ref):
    tiles = fields.shape[1]
    sub = lax.broadcasted_iota(jnp.int32, (8, LANES), 0)
    for pair in range(FIELDS // 2):
        for t in range(tiles):
            even, odd = fields.at[2 * pair, t], fields.at[2 * pair + 1, t]
            up_ref[pair * tiles + t] = jnp.where(sub < HALO, even[:EDGE], pltpu.roll(odd[:EDGE], HALO, 0))
            down_ref[pair * tiles + t] = jnp.where(sub < HALO, pltpu.roll(odd[-EDGE:], HALO, 0), even[-EDGE:])
    lane = lax.broadcasted_iota(jnp.int32, (8, LANES), 1)
    base = FIELDS // 2 * tiles
    for index, strip in enumerate((from_left, own_left, own_right, from_right)):
        packed = jnp.zeros((8, LANES), F32)
        for field in range(FIELDS):
            turned = pltpu.roll(strip[field], 8 * field, 1) if field else strip[field]
            place = (lane - 8 * field + HALO) % LANES
            packed = jnp.where(place < 2 * HALO, turned, packed)
        up_ref[base + index] = packed
        down_ref[base + index] = packed
    up_ref[base + 4] = steps[1, :8]
    down_ref[base + 4] = steps[1, :8]


def pack_rows(fields, steps, strips):
    shape = jax.ShapeDtypeStruct((FIELDS // 2 * fields.shape[1] + 5, 8, LANES), F32)
    return in_vmem(rows_kernel, "pack_rows", [shape, shape])(fields, steps, *strips)


def edges_kernel(place_ref, fields, steps, *refs):
    own_left, own_right, from_left, from_right, from_above, from_below, out_ref = refs[:7]
    row_strip, col_strip, row_step, row_grad, col_grad, row_keep, col_keep = refs[7:]
    tiles = fields.shape[1]
    base = FIELDS // 2 * tiles
    has_above, has_below, has_left, has_right = (place_ref[i] for i in range(4))
    lane = lax.broadcasted_iota(jnp.int32, (8, LANES), 1)
    sub = lax.broadcasted_iota(jnp.int32, (8, LANES), 0)

    corners = [
        jnp.where((lane % 8) < HALO, from_below[base + index], from_above[base + index]) for index in range(4)
    ]
    beside = [[None] * 4 for _ in range(FIELDS)]
    for field in range(FIELDS):
        for index, strip in enumerate((from_left, own_left, own_right, from_right)):
            value = strip[field]
            outer = pltpu.roll(corners[index], (LANES - 8 * field) % LANES, 1) if field else corners[index]
            if field == LAND:
                outer = outer * jnp.where(lane < LANES // 2, has_below, has_above)
                if index == 0:
                    value, outer = value * has_left, outer * has_left
                if index == 3:
                    value, outer = value * has_right, outer * has_right
            col_strip[field, 0, 8 * index : 8 * index + 8, :] = value
            col_strip[field, 1, 8 * index : 8 * index + 8, :] = outer
            beside[field][index] = (value, outer)

    def lined(value, outer):
        out = jnp.where(lane < 8, pltpu.roll(outer, 8, 1), pltpu.roll(value, 8, 1))
        out = jnp.where(lane < 16, out, pltpu.roll(value, 24, 1))
        return jnp.where(lane < 24, out, pltpu.roll(outer, 24, 1))

    zeros = jnp.zeros((8, LANES), F32)
    stack = []
    for index in range(LANES // 8):
        here = lined(*beside[index][3]) if index < FIELDS else zeros
        following = (index + 1) % (LANES // 8)
        after = lined(*beside[following][0]) if following < FIELDS else zeros
        stack.append(jnp.where(sub < HALO, here, after))
    flipped = jnp.transpose(jnp.concatenate(stack, 0))[:32]
    own_step = steps[1, :8]
    outer_step = jnp.where(lane < LANES // 2, from_below[base + 4], from_above[base + 4])
    row_step[...] = step_rows(lined(own_step, outer_step))[:32]
    for field in range(FIELDS):
        for t in range(tiles):
            above, below = from_above[field // 2 * tiles + t], from_below[field // 2 * tiles + t]
            if field % 2:
                above, below = pltpu.roll(above, HALO, 0), pltpu.roll(below, HALO, 0)
            if field == LAND:
                above, below = above * has_above, below * has_below
            own = fields.at[field, t]
            for index, value in enumerate((above, own[:EDGE], own[-EDGE:], below)):
                row_strip[field, t, 8 * index : 8 * index + 8, :] = value
        row_strip[field, tiles] = pltpu.roll(flipped, (LANES - 8 * field) % LANES, 1) if field else flipped

    slabs = 3
    for strip, grad, kept, count in (
        (row_strip, row_grad, row_keep, tiles + 1),
        (col_strip, col_grad, col_keep, 2),
    ):
        on_rows = strip is row_strip

        def load(field, k):
            parts = [strip[field, t, pl.ds(HALO + k, 8, stride=slabs), :] for t in range(count)]
            return jnp.stack(parts)

        def steps_at(k):
            if on_rows:
                part = row_step[pl.ds(HALO + k, 8, stride=slabs), :]
                return jnp.broadcast_to(part[None], (count, 8, LANES))
            return jnp.stack([own_step, outer_step])

        def put(which, k, value):
            for t in range(count):
                grad[which, t, pl.ds(HALO + k, 8, stride=slabs), :] = value[t]

        keep = {name: kept.at[index] for index, name in enumerate(SAVED)}
        dynamics(slabs, slabs, count, load, steps_at, keep, put)
    for which in range(2):
        for t in range(tiles):
            out_ref[which, :, t * LANES : (t + 1) * LANES] = jnp.where(
                sub < HALO, row_grad[which, t, 8:16, :], row_grad[which, t, 16:24, :]
            )
        out_ref[which, :, tiles * LANES :] = jnp.where(
            sub < HALO, col_grad[which, 0, 8:16, :], col_grad[which, 0, 16:24, :]
        )


def edges(place, fields, steps, strips, from_above, from_below):
    tiles = fields.shape[1]
    scratch = [
        pltpu.VMEM((FIELDS, tiles + 1, 32, LANES), F32),
        pltpu.VMEM((FIELDS, 2, 32, LANES), F32),
        pltpu.VMEM((32, LANES), F32),
        pltpu.VMEM((2, tiles + 1, 32, LANES), F32),
        pltpu.VMEM((2, 2, 32, LANES), F32),
        pltpu.VMEM((len(SAVED), 4, tiles + 1, 8, LANES), F32),
        pltpu.VMEM((len(SAVED), 4, 2, 8, LANES), F32),
    ]
    operands = [place, fields, steps, *strips, from_above, from_below]
    space = pl.BlockSpec(memory_space=pltpu.VMEM)
    return pl.pallas_call(
        edges_kernel,
        out_shape=jax.ShapeDtypeStruct((2, EDGE, (tiles + 1) * LANES), F32),
        in_specs=[pl.BlockSpec(memory_space=pltpu.SMEM)] + [space] * (len(operands) - 1),
        out_specs=space,
        scratch_shapes=scratch,
        cost_estimate=cost(EDGES_US),
        compiler_params=pltpu.CompilerParams(vmem_limit_bytes=VMEM_BYTES),
        name="edges",
    )(*operands)


def update_kernel(parts, terms, maps_ref, first_ref, second_ref, *refs):
    grads, edge_refs = refs[: parts * terms], refs[parts * terms : (parts + 1) * terms]
    new_maps, new_first, new_second = refs[(parts + 1) * terms :]
    rows, columns = maps_ref.shape[1:]
    tiles = columns // LANES
    lane = lax.broadcasted_iota(jnp.int32, (rows, LANES), 1)
    sub = lax.broadcasted_iota(jnp.int32, (EDGE, LANES), 0)
    edge = sum(ref[...] for ref in edge_refs)
    strips = [edge[which, :, columns:] for which in range(2)]
    blank = jnp.zeros((LANES - 2 * EDGE, LANES), F32)
    flipped = jnp.transpose(jnp.concatenate([*strips, blank], 0))
    height = rows // parts
    for which in range(2):
        for t in range(tiles):
            own = slice(t * LANES, (t + 1) * LANES)
            grad = jnp.concatenate(
                [sum(ref[which, :, own] for ref in grads[part * terms : (part + 1) * terms]) for part in range(parts)],
                0,
            )
            outer = edge[which, :, own]
            grad = jnp.concatenate(
                [
                    jnp.where(sub < HALO, outer, grad[:EDGE]),
                    grad[EDGE:-EDGE],
                    jnp.where(sub < HALO, grad[-EDGE:], outer),
                ],
                0,
            )
            if t == 0:
                beside = pltpu.roll(flipped, LANES - EDGE * which, 1) if which else flipped
                grad = jnp.where(lane < HALO, beside, grad)
            if t == tiles - 1:
                beside = pltpu.roll(flipped, LANES - EDGE * (which + 1), 1)
                grad = jnp.where(lane >= LANES - HALO, beside, grad)
            first = BETA_FIRST * first_ref[which, :, own] + (1.0 - BETA_FIRST) * grad
            second = BETA_SECOND * second_ref[which, :, own] + (1.0 - BETA_SECOND) * grad * grad
            new_first[which, :, own] = first
            new_second[which, :, own] = second
            scale = jnp.sqrt(second * (1.0 / (1.0 - BETA_SECOND**ADAM_STEP))) + ADAM_EPS
            change = (LEARN_RATE / (1.0 - BETA_FIRST**ADAM_STEP)) * first
            new_maps[which, :, own] = maps_ref[which, :, own] - change * reciprocal(scale)


def update(maps, first_moment, second_moment, grads, edge_grads):
    parts, terms = len(grads), len(edge_grads)
    flat = [term for grad in grads for term in grad]
    shape = jax.ShapeDtypeStruct(maps.shape, F32)
    kernel = functools.partial(update_kernel, parts, terms)
    return in_vmem(kernel, "update", [shape] * 3)(maps, first_moment, second_moment, *flat, *edge_grads)


def shifts(axis):
    count = lax.axis_size(axis)
    forward = [(i, (i + 1) % count) for i in range(count)]
    return forward, [(target, source) for source, target in forward]


def both_scenarios(value):
    count = lax.axis_size("scen")
    if count == 2:
        return [value, lax.ppermute(value, "scen", [(0, 1), (1, 0)])]
    return [lax.psum(value, "scen")]


def shards(
    density,
    trait,
    variance,
    optimum,
    observed,
    obs_step,
    land_code,
    maps,
    first_moment,
    second_moment,
):
    sources = (density, trait, variance, optimum, observed, land_code, maps)
    rows = maps.shape[1]
    middle = rows // 2
    fields, steps, own_left, own_right = load_tile(sources, obs_step)
    rightward, leftward = shifts("ly")
    from_left = lax.ppermute(own_right, "ly", rightward)
    from_right = lax.ppermute(own_left, "ly", leftward)
    upper_terms = both_scenarios(window(0, middle + EDGE, 0, middle, fields, steps))
    strips = (own_left, own_right, from_left, from_right)
    up, down = pack_rows(fields, steps, strips)
    downward, upward = shifts("lx")
    from_above = lax.ppermute(down, "lx", downward)
    from_below = lax.ppermute(up, "lx", upward)
    lower = window(middle - EDGE, middle + EDGE, middle, middle, fields, steps, *strips, up, down)
    lower_terms = both_scenarios(lower)
    row, column = lax.axis_index("lx"), lax.axis_index("ly")
    place = jnp.stack(
        [row > 0, row < lax.axis_size("lx") - 1, column > 0, column < lax.axis_size("ly") - 1]
    ).astype(F32)
    outer = edges(place, fields, steps, strips, from_above, from_below)
    outer_terms = both_scenarios(outer)
    return tuple(update(maps, first_moment, second_moment, [upper_terms, lower_terms], outer_terms))


def solution(mesh):
    in_specs = (
        P("scen", "lx", "ly"),
        P("scen", "lx", "ly"),
        P("scen", "lx", "ly"),
        P("scen", "lx", "ly"),
        P("scen", "lx", "ly"),
        P("scen", "lx"),
        P("lx", "ly"),
        P(None, "lx", "ly"),
        P(None, "lx", "ly"),
        P(None, "lx", "ly"),
    )
    out_specs = (P(None, "lx", "ly"), P(None, "lx", "ly"), P(None, "lx", "ly"))
    return jax.shard_map(shards, mesh=mesh, in_specs=in_specs, out_specs=out_specs, check_vma=False)
```

```python
import functools

import jax
import jax.numpy as jnp
from jax import lax
from jax.experimental import pallas as pl
from jax.experimental.pallas import tpu as pltpu
from jax.sharding import PartitionSpec as P

STEPS = 2
ADAM_STEP = 10
REACH_MAX = 0.2
PRIOR_WEIGHT = 0.1
GROWTH_RATE = 0.5
MUTATION_INPUT = 0.02
LEARN_RATE = 0.01
BETA_FIRST = 0.9
BETA_SECOND = 0.999
ADAM_EPS = 1e-08
LOSS_WEIGHT = 2.0

F32 = jnp.float32
LANES = 128
EDGE = 8
HALO = 4
DENSITY, TRAIT, VARIANCE, DISPERSAL, SELECTION, OPTIMUM, LAND, OBSERVED = range(8)
FIELDS = 8
RINGS = True, False
GROUPS = {5: (5, 5, 5, 5, 5, 5), 9: (9, 9, 3, 3, 3, 9)}
CUTS = (32, 96)
WINDOW_US, EDGES_US = 4, 20
VMEM_BYTES = 16 * 1024 * 1024
SAVED = (
    "half",
    "land",
    "select",
    "n0",
    "q0",
    "m0",
    "wd",
    "wr",
    "lr",
    "dr0n",
    "dr0q",
    "dr0m",
    "e",
    "d",
    "vs",
    "p",
    "zs",
    "r",
    "n1",
    "q1",
    "m1",
    "z1",
    "u1",
    "dr1n",
    "dr1q",
    "dr1m",
    "a2n",
    "a2q",
    "a2m",
    "gsel",
    "gd",
    "gr",
    "a1n",
    "a1q",
    "a1m",
)


def cost(microseconds):
    return pl.CostEstimate(flops=int(microseconds * 1e9), transcendentals=0, bytes_accessed=int(microseconds * 3.6e6))


def reciprocal(value):
    guess = pl.reciprocal(value, approx=True)
    return guess * (2.0 - value * guess)


def sigmoid(value):
    return 0.5 + 0.5 * jnp.tanh(0.5 * value)


def dynamics(slabs, groups, cycles, load, steps_at, keep, put):
    lane = lax.broadcasted_iota(jnp.int32, (sum(cycles), 8, LANES), 2)
    at_last, at_first = lane == LANES - 1, lane == 0

    def turn_tiles(value, by):
        parts, start = [], 0
        for count in cycles:
            cut = start + by % count
            parts += [value[cut : start + count], value[start:cut]]
            start += count
        return jnp.concatenate([part for part in parts if part.shape[0]], 0)

    def right(value):
        turned = pltpu.roll(value, LANES - 1, 2)
        return jnp.where(at_last, turn_tiles(turned, 1), turned)

    def left(value):
        turned = pltpu.roll(value, 1, 2)
        return jnp.where(at_first, turn_tiles(turned, -1), turned)

    def each_slab(stage, body, carry=()):
        group = groups[stage]

        def step(index, carry):
            for offset in range(group):
                carry = body(index * group + offset, carry)
            return carry

        if group == slabs:
            return step(0, carry)
        return lax.fori_loop(0, slabs // group, step, carry)

    def close(names):
        for name in names:
            keep[name][slabs] = pltpu.roll(keep[name][0], 7, 1)

    def wrapped(values):
        return tuple(pltpu.roll(value, 1, 1) for value in values)

    def down_gap(name, k):
        return keep[name][k + 1] - keep[name][k]

    def row_fluxes(names, k):
        weight = keep["wd"][k]
        gaps = [down_gap(name, k) for name in names]
        return gaps, tuple(weight * gap for gap in gaps)

    def spread(names, k, above):
        row_gaps, row_flux = row_fluxes(names, k)
        weight = keep["wr"][k]
        out, col_gaps = [], []
        for name, flux, before in zip(names, row_flux, above):
            value = keep[name][k]
            gap = right(value) - value
            col_flux = weight * gap
            out.append(value + (flux - before) + (col_flux - left(col_flux)))
            col_gaps.append(gap)
        return out, row_gaps, col_gaps, row_flux

    def begin(k, _):
        keep["half"][k] = 0.5 * REACH_MAX * sigmoid(load(DISPERSAL, k))
        keep["land"][k] = load(LAND, k)
        raw = load(SELECTION, k)
        keep["select"][k] = jnp.maximum(raw, 0.0) + jnp.log(1.0 + jnp.exp(-jnp.abs(raw)))
        n, z, v = load(DENSITY, k), load(TRAIT, k), load(VARIANCE, k)
        keep["n0"][k] = n
        keep["q0"][k] = n * z
        keep["m0"][k] = n * (v + z * z)
        return ()

    each_slab(0, begin)
    close(("half", "land", "n0", "q0", "m0"))

    def weigh(k, _):
        half, land = keep["half"][k], keep["land"][k]
        keep["wd"][k] = (half + keep["half"][k + 1]) * (land * keep["land"][k + 1])
        pair = land * right(land)
        keep["lr"][k] = pair
        keep["wr"][k] = (half + right(half)) * pair
        return ()

    each_slab(1, weigh)
    first_names, second_names = ("n0", "q0", "m0"), ("n1", "q1", "m1")

    def first_step(k, above):
        (ns, qs, ms), _, col_gaps, above = spread(first_names, k, above)
        for name, gap in zip(("dr0n", "dr0q", "dr0m"), col_gaps):
            keep[name][k] = gap
        z, v = load(TRAIT, k), load(VARIANCE, k)
        optimum, select, land = load(OPTIMUM, k), keep["select"][k], keep["land"][k]
        r = reciprocal(ns + PRIOR_WEIGHT)
        zs = (qs + PRIOR_WEIGHT * z) * r
        vs = (ms + PRIOR_WEIGHT * (v + z * z)) * r - zs * zs
        d = zs - optimum
        p = reciprocal(1.0 + select * vs)
        e = jnp.exp(land * (GROWTH_RATE * (1.0 - ns) - 0.5 * select * (d * d + vs)))
        n1 = ns * e
        z1 = optimum + p * d
        u1 = vs * p + MUTATION_INPUT + z1 * z1
        for name, value in zip(
            ("e", "d", "vs", "p", "zs", "r", "n1", "q1", "m1", "z1", "u1"),
            (e, d, vs, p, zs, r, n1, n1 * z1, n1 * u1, z1, u1),
        ):
            keep[name][k] = value
        return above

    each_slab(2, first_step, wrapped(row_fluxes(first_names, slabs - 1)[1]))
    close(second_names)

    def second_step(k, above):
        (ns, qs, ms), _, col_gaps, above = spread(second_names, k, above)
        for name, gap in zip(("dr1n", "dr1q", "dr1m"), col_gaps):
            keep[name][k] = gap
        optimum, select, land = load(OPTIMUM, k), keep["select"][k], keep["land"][k]
        r = reciprocal(ns + PRIOR_WEIGHT)
        zs = (qs + PRIOR_WEIGHT * keep["z1"][k]) * r
        es = (ms + PRIOR_WEIGHT * keep["u1"][k]) * r
        vs = es - zs * zs
        d = zs - optimum
        misfit = d * d + vs
        e = jnp.exp(land * (GROWTH_RATE * (1.0 - ns) - 0.5 * select * misfit))
        n2 = ns * e
        weight = jnp.where(steps_at(k) == 2.0, 2.0 * LOSS_WEIGHT * land, 0.0)
        an = weight * (n2 - load(OBSERVED, k))
        b = 0.5 * an * n2
        av = -b * select
        am = av * r
        aq = -2.0 * optimum * am
        keep["gsel"][k] = -b * misfit
        keep["a2n"][k] = an * e - b - (aq * zs + am * es)
        keep["a2q"][k] = aq
        keep["a2m"][k] = am
        return above

    each_slab(3, second_step, wrapped(row_fluxes(second_names, slabs - 1)[1]))
    second_back, first_back = ("a2n", "a2q", "a2m"), ("a1n", "a1q", "a1m")
    close(second_back)

    def back(k, above):
        (an, aq, am), row_gaps, col_gaps, above = spread(second_back, k, above)
        n_gap, q_gap, m_gap = [down_gap(name, k) * gap for name, gap in zip(second_names, row_gaps)]
        keep["gd"][k] = n_gap + q_gap + m_gap
        n_gap, q_gap, m_gap = [keep[f][k] * gap for f, gap in zip(("dr1n", "dr1q", "dr1m"), col_gaps)]
        keep["gr"][k] = n_gap + q_gap + m_gap
        n1, z1, land, select = keep["n1"][k], keep["z1"][k], keep["land"][k], keep["select"][k]
        e, d, vs, p, zs, r = (keep[name][k] for name in ("e", "d", "vs", "p", "zs", "r"))
        av = PRIOR_WEIGHT * keep["a2m"][k] + am * n1
        az = PRIOR_WEIGHT * keep["a2q"][k] + aq * n1 + 2.0 * z1 * av
        weight = jnp.where(steps_at(k) == 1.0, 2.0 * LOSS_WEIGHT * land, 0.0)
        an = an + aq * z1 + am * keep["u1"][k] + weight * (n1 - load(OBSERVED, k))
        b = 0.5 * an * n1 * land
        at = -(az * d + av * vs) * (p * p)
        gsel = keep["gsel"][k] + at * vs - b * (d * d + vs)
        avs = av * p + select * (at - b)
        azs = az * p - 2.0 * (b * select * d + zs * avs)
        aqs, ams = azs * r, avs * r
        keep["a1n"][k] = an * e - b - (aqs * zs + ams * (vs + zs * zs))
        keep["a1q"][k] = aqs
        keep["a1m"][k] = ams
        put(1, k, gsel * sigmoid(load(SELECTION, k)))
        return above

    each_slab(4, back, wrapped(row_fluxes(second_back, slabs - 1)[1]))
    close(first_back)

    def row_share(k):
        n_gap, q_gap, m_gap = [down_gap(a, k) * down_gap(f, k) for a, f in zip(first_back, first_names)]
        return (keep["gd"][k] + n_gap + q_gap + m_gap) * (keep["land"][k] * keep["land"][k + 1])

    def finish(k, above):
        here = row_share(k)
        total = keep["gr"][k]
        for name, field in zip(first_back, ("dr0n", "dr0q", "dr0m")):
            value = keep[name][k]
            total = total + (right(value) - value) * keep[field][k]
        total = total * keep["lr"][k]
        half = keep["half"][k]
        put(0, k, half * (10.0 * half - 1.0) * (here + above[0] + total + left(total)))
        return (here,)

    each_slab(5, finish, wrapped((row_share(slabs - 1),)))


def step_rows(line):
    return jnp.transpose(jnp.concatenate([line] * (LANES // 8), 0))


def tile_copies(tiles, first, rows, sources, fields, codes, sems):
    density, trait, variance, optimum, observed, land_code, maps = sources
    moves = (
        (maps, fields.at[DISPERSAL : SELECTION + 1]),
        (land_code, codes),
        (density.at[0], fields.at[DENSITY]),
        (trait.at[0], fields.at[TRAIT]),
        (variance.at[0], fields.at[VARIANCE]),
        (optimum.at[0], fields.at[OPTIMUM]),
        (observed.at[0], fields.at[OBSERVED]),
    )
    part = pl.ds(first, rows)
    copies = []
    for index, (source, target) in enumerate(moves):
        for t in range(tiles):
            lanes = pl.ds(t * LANES, LANES)
            if source is maps:
                ends = source.at[:, part, lanes], target.at[:, t, part]
            else:
                ends = source.at[part, lanes], target.at[t, part]
            copies.append(pltpu.make_async_copy(*ends, sems.at[index, t]))
    return copies


def window_kernel(first, rows, skip, fields, steps, *refs):
    out_ref, grads, kept = refs[-3:]
    tiles = fields.shape[1]
    out_rows = out_ref.shape[1]
    slabs = rows // 8

    def load(field, k):
        return jnp.stack([fields[field, t, pl.ds(first + k, 8, stride=slabs), :] for t in range(tiles)])

    def steps_at(k):
        part = steps[0, pl.ds(first + k, 8, stride=slabs), :]
        return jnp.broadcast_to(part[None], (tiles, 8, LANES))

    def put(which, k, value):
        for t in range(tiles):
            grads[which, t, pl.ds(k, 8, stride=slabs), :] = value[t]

    keep = {name: kept.at[index] for index, name in enumerate(SAVED)}
    dynamics(slabs, GROUPS[slabs], (tiles,), load, steps_at, keep, put)
    for which in range(2):
        for t in range(tiles):
            out_ref[which, :, t * LANES : (t + 1) * LANES] = grads[which, t, skip : skip + out_rows, :]


def first_kernel(tiles, rows, *refs):
    sources, step_ref = refs[:7], refs[7]
    out_ref, fields, steps, pair_ref, other_ref, codes, line, grads, kept, sems, late_sems = refs[8:]
    height = fields.shape[2]
    early = tile_copies(tiles, 0, rows, sources, fields, codes, sems)
    late = tile_copies(tiles, rows, height - rows, sources, fields, codes, late_sems)
    early.append(pltpu.make_async_copy(step_ref, line, sems.at[7, 0]))
    for copy in early + late:
        copy.start()
    for copy in early:
        copy.wait()
    fields[LAND, :, :rows] = codes[:, :rows].astype(F32)
    wide = jnp.broadcast_to(line[0:1, :].astype(F32), (8, LANES))
    steps[0] = step_rows(wide)
    steps[1] = jnp.broadcast_to(wide[0:1], (LANES, LANES))
    window_kernel(0, rows, 0, fields, steps, out_ref, grads, kept)
    for copy in late:
        copy.wait()
    fields[LAND, :, rows:] = codes[:, rows:].astype(F32)
    columns_kernel(fields, pair_ref, other_ref)


def first_window(rows, out_rows, sources, obs_step):
    height, columns = sources[0].shape[1:]
    tiles = columns // LANES
    strip = jax.ShapeDtypeStruct((FIELDS, EDGE, height), F32)
    return pl.pallas_call(
        functools.partial(first_kernel, tiles, rows),
        out_shape=[
            jax.ShapeDtypeStruct((2, out_rows, columns), F32),
            jax.ShapeDtypeStruct((FIELDS, tiles, height, LANES), F32),
            jax.ShapeDtypeStruct((2, LANES, LANES), F32),
            strip,
            strip,
        ],
        in_specs=[pl.BlockSpec(memory_space=pltpu.HBM)] * 8,
        out_specs=[pl.BlockSpec(memory_space=pltpu.VMEM)] * 5,
        scratch_shapes=[
            pltpu.VMEM((tiles, height, LANES), jnp.int32),
            pltpu.VMEM(obs_step.shape, jnp.int32),
            pltpu.VMEM((2, tiles, rows, LANES), F32),
            pltpu.VMEM((len(SAVED), rows // 8 + 1, tiles, 8, LANES), F32),
            pltpu.SemaphoreType.DMA((8, tiles)),
            pltpu.SemaphoreType.DMA((7, tiles)),
        ],
        cost_estimate=cost(WINDOW_US),
        compiler_params=pltpu.CompilerParams(vmem_limit_bytes=VMEM_BYTES),
        name="first_window",
    )(*(pltpu.with_memory_space_constraint(source, pltpu.HBM) for source in (*sources, obs_step)))


def window(first, rows, out_first, out_rows, fields, steps, *after):
    tiles = fields.shape[1]
    return pl.pallas_call(
        functools.partial(window_kernel, first, rows, out_first - first),
        out_shape=jax.ShapeDtypeStruct((2, out_rows, tiles * LANES), F32),
        in_specs=[pl.BlockSpec(memory_space=pltpu.VMEM)] * 2 + [pl.BlockSpec(memory_space=pltpu.VMEM)] * len(after),
        out_specs=pl.BlockSpec(memory_space=pltpu.VMEM),
        scratch_shapes=[
            pltpu.VMEM((2, tiles, rows, LANES), F32),
            pltpu.VMEM((len(SAVED), rows // 8 + 1, tiles, 8, LANES), F32),
        ],
        cost_estimate=cost(WINDOW_US),
        compiler_params=pltpu.CompilerParams(vmem_limit_bytes=VMEM_BYTES),
        name=f"window_{out_first}",
    )(fields, steps, *after)


def columns_kernel(fields, pair_ref, other_ref):
    rightward = is_even("ly")
    tiles, rows = fields.shape[1:3]
    lane = lax.broadcasted_iota(jnp.int32, (rows, LANES), 1)
    packed = jnp.zeros((rows, LANES), F32)
    for field in range(FIELDS):
        both = jnp.where(lane < EDGE, fields[field, 0], fields[field, tiles - 1])
        turned = pltpu.roll(both, 16 * field, 1) if field else both
        place = (lane - 16 * field + EDGE) % LANES
        packed = jnp.where(place < 2 * EDGE, turned, packed)
    flipped = jnp.transpose(packed)
    for field in range(FIELDS):
        left = flipped[16 * field : 16 * field + EDGE]
        start = (16 * field - EDGE) % LANES
        right = flipped[start : start + EDGE]
        pair_ref[field] = jnp.where(rightward, right, left)
        other_ref[field] = jnp.where(rightward, left, right)


def in_vmem(kernel, name, out_shape):
    def call(*operands):
        many = isinstance(out_shape, (list, tuple))
        space = pl.BlockSpec(memory_space=pltpu.VMEM)
        return pl.pallas_call(
            kernel,
            out_shape=out_shape,
            in_specs=[space] * len(operands),
            out_specs=[space] * len(out_shape) if many else space,
            compiler_params=pltpu.CompilerParams(vmem_limit_bytes=VMEM_BYTES),
            name=name,
        )(*operands)

    return call


def is_even(axis):
    return lax.axis_index(axis) % 2 == 0


def present(axis):
    place = lax.axis_index(axis)
    return (place > 0).astype(F32), (place < lax.axis_size(axis) - 1).astype(F32)


def chosen(which, one, other):
    return lambda index: jnp.where(which, one[index], other[index])


def rows_kernel(fields, steps, from_pair, from_other, pair_ref, other_ref):
    tiles = fields.shape[1]
    downward, rightward = is_even("lx"), is_even("ly")
    sub = lax.broadcasted_iota(jnp.int32, (8, LANES), 0)
    for pair in range(FIELDS // 2):
        for t in range(tiles):
            even, odd = fields.at[2 * pair, t], fields.at[2 * pair + 1, t]
            up = jnp.where(sub < HALO, even[:EDGE], pltpu.roll(odd[:EDGE], HALO, 0))
            down = jnp.where(sub < HALO, pltpu.roll(odd[-EDGE:], HALO, 0), even[-EDGE:])
            pair_ref[pair * tiles + t] = jnp.where(downward, down, up)
            other_ref[pair * tiles + t] = jnp.where(downward, up, down)
    lane = lax.broadcasted_iota(jnp.int32, (8, LANES), 1)
    base = FIELDS // 2 * tiles
    strips = chosen(rightward, from_other, from_pair), chosen(rightward, from_pair, from_other)
    for index, strip in enumerate(strips):
        packed = jnp.zeros((8, LANES), F32)
        for field in range(FIELDS):
            turned = pltpu.roll(strip(field), 8 * field, 1) if field else strip(field)
            place = (lane - 8 * field + HALO) % LANES
            packed = jnp.where(place < 2 * HALO, turned, packed)
        pair_ref[base + index] = packed
        other_ref[base + index] = packed
    pair_ref[base + 2] = steps[1, :8]
    other_ref[base + 2] = steps[1, :8]


def pack_rows(*operands):
    fields = operands[0]
    shape = jax.ShapeDtypeStruct((FIELDS // 2 * fields.shape[1] + 3, 8, LANES), F32)
    return in_vmem(rows_kernel, "pack_rows", [shape, shape])(*operands)


def outer_rows(grad, which, t):
    sub = lax.broadcasted_iota(jnp.int32, (8, LANES), 0)
    return jnp.where(sub < HALO, grad[which, t, 8:16, :], grad[which, t, 16:24, :])


def edges_kernel(fields, steps, own_pair, own_other, side_pair, side_other, end_pair, end_other, *refs):
    out_ref, strip, grad, kept, row_step = refs
    tiles = fields.shape[1]
    base = FIELDS // 2 * tiles
    (has_above, has_below), (has_left, has_right) = present("lx"), present("ly")
    downward, rightward = is_even("lx"), is_even("ly")
    own_left, own_right = chosen(rightward, own_other, own_pair), chosen(rightward, own_pair, own_other)
    from_left, from_right = chosen(rightward, side_other, side_pair), chosen(rightward, side_pair, side_other)
    from_above, from_below = chosen(downward, end_other, end_pair), chosen(downward, end_pair, end_other)
    lane = lax.broadcasted_iota(jnp.int32, (8, LANES), 1)
    sub = lax.broadcasted_iota(jnp.int32, (8, LANES), 0)
    within = jnp.where(lane < LANES // 2, has_below, has_above)

    def lined(value, outer):
        out = jnp.where(lane < 8, pltpu.roll(outer, 8, 1), pltpu.roll(value, 8, 1))
        out = jnp.where(lane < 16, out, pltpu.roll(value, 24, 1))
        return jnp.where(lane < 24, out, pltpu.roll(outer, 24, 1))

    def beside(side, index, present):
        corners = jnp.where((lane % 8) < HALO, from_below(base + index), from_above(base + index))
        out = []
        for field in range(FIELDS):
            value = side(field)
            outer = pltpu.roll(corners, (LANES - 8 * field) % LANES, 1) if field else corners
            if field == LAND:
                value, outer = value * present, outer * (within * present)
            out.append(lined(value, outer))
        return out

    lefts, rights = beside(from_left, 0, has_left), beside(from_right, 1, has_right)
    zeros = jnp.zeros((8, LANES), F32)
    stack = []
    for index in range(LANES // 8):
        following = (index + 1) % (LANES // 8)
        here = rights[index] if index < FIELDS else zeros
        after = lefts[following] if following < FIELDS else zeros
        stack.append(jnp.where(sub < HALO, here, after))
    flipped = jnp.transpose(jnp.concatenate(stack, 0))[:32]
    outer_step = jnp.where(lane < LANES // 2, from_below(base + 2), from_above(base + 2))
    row_step[...] = step_rows(lined(steps[1, :8], outer_step))[:32]
    for field in range(FIELDS):
        for t in range(tiles):
            above, below = from_above(field // 2 * tiles + t), from_below(field // 2 * tiles + t)
            if field % 2:
                above, below = pltpu.roll(above, HALO, 0), pltpu.roll(below, HALO, 0)
            if field == LAND:
                above, below = above * has_above, below * has_below
            own = fields.at[field, t]
            for index, value in enumerate((above, own[:EDGE], own[-EDGE:], below)):
                strip[field, t, 8 * index : 8 * index + 8, :] = value
        strip[field, tiles] = pltpu.roll(flipped, (LANES - 8 * field) % LANES, 1) if field else flipped
        left, right = from_left(field), from_right(field)
        if field == LAND:
            left, right = left * has_left, right * has_right
        for index, value in enumerate((left, own_left(field), own_right(field), right)):
            strip[field, tiles + 1, 8 * index : 8 * index + 8, :] = value

    slabs = 3
    count = tiles + 2

    def load(field, k):
        return jnp.stack([strip[field, t, pl.ds(HALO + k, 8, stride=slabs), :] for t in range(count)])

    def steps_at(k):
        part = row_step[pl.ds(HALO + k, 8, stride=slabs), :]
        return jnp.stack([part] * (tiles + 1) + [steps[1, :8]])

    def put(which, k, value):
        for t in range(count):
            grad[which, t, pl.ds(HALO + k, 8, stride=slabs), :] = value[t]

    keep = {name: kept.at[index] for index, name in enumerate(SAVED)}
    dynamics(slabs, (slabs,) * 6, (tiles + 1, 1), load, steps_at, keep, put)
    for which in range(2):
        for t in range(tiles):
            out_ref[which, :, t * LANES : (t + 1) * LANES] = outer_rows(grad, which, t)
        out_ref[which, :, tiles * LANES :] = outer_rows(grad, which, tiles + 1)


def edges(fields, steps, *strips):
    tiles = fields.shape[1]
    count = tiles + 2
    space = pl.BlockSpec(memory_space=pltpu.VMEM)
    operands = [fields, steps, *strips]
    return pl.pallas_call(
        edges_kernel,
        out_shape=jax.ShapeDtypeStruct((2, EDGE, (tiles + 1) * LANES), F32),
        in_specs=[space] * len(operands),
        out_specs=space,
        scratch_shapes=[
            pltpu.VMEM((FIELDS, count, 32, LANES), F32),
            pltpu.VMEM((2, count, 32, LANES), F32),
            pltpu.VMEM((len(SAVED), 4, count, 8, LANES), F32),
            pltpu.VMEM((32, LANES), F32),
        ],
        cost_estimate=cost(EDGES_US),
        compiler_params=pltpu.CompilerParams(vmem_limit_bytes=VMEM_BYTES),
        name="edges",
    )(*operands)


def update_kernel(parts, terms, maps_ref, first_ref, second_ref, *refs):
    grads, edge_refs = refs[: parts * terms], refs[parts * terms : (parts + 1) * terms]
    new_maps, new_first, new_second = refs[(parts + 1) * terms :]
    rows, columns = maps_ref.shape[1:]
    tiles = columns // LANES
    lane = lax.broadcasted_iota(jnp.int32, (rows, LANES), 1)
    sub = lax.broadcasted_iota(jnp.int32, (EDGE, LANES), 0)
    edge = sum(ref[...] for ref in edge_refs)
    strips = [edge[which, :, columns:] for which in range(2)]
    blank = jnp.zeros((LANES - 2 * EDGE, LANES), F32)
    flipped = jnp.transpose(jnp.concatenate([*strips, blank], 0))
    for which in range(2):
        for t in range(tiles):
            own = slice(t * LANES, (t + 1) * LANES)
            grad = jnp.concatenate(
                [sum(ref[which, :, own] for ref in grads[part * terms : (part + 1) * terms]) for part in range(parts)],
                0,
            )
            if t == 0:
                beside = pltpu.roll(flipped, LANES - EDGE * which, 1) if which else flipped
                grad = jnp.where(lane < HALO, beside, grad)
            if t == tiles - 1:
                beside = pltpu.roll(flipped, LANES - EDGE * (which + 1), 1)
                grad = jnp.where(lane >= LANES - HALO, beside, grad)
            outer = edge[which, :, own]
            grad = jnp.concatenate(
                [
                    jnp.where(sub < HALO, outer, grad[:EDGE]),
                    grad[EDGE:-EDGE],
                    jnp.where(sub < HALO, grad[-EDGE:], outer),
                ],
                0,
            )
            first = BETA_FIRST * first_ref[which, :, own] + (1.0 - BETA_FIRST) * grad
            second = BETA_SECOND * second_ref[which, :, own] + (1.0 - BETA_SECOND) * grad * grad
            new_first[which, :, own] = first
            new_second[which, :, own] = second
            scale = jnp.sqrt(second * (1.0 / (1.0 - BETA_SECOND**ADAM_STEP))) + ADAM_EPS
            change = (LEARN_RATE / (1.0 - BETA_FIRST**ADAM_STEP)) * first
            new_maps[which, :, own] = maps_ref[which, :, own] - change * reciprocal(scale)


def update(maps, first_moment, second_moment, grads, edge_grads):
    parts, terms = len(grads), len(edge_grads)
    flat = [term for grad in grads for term in grad]
    shape = jax.ShapeDtypeStruct(maps.shape, F32)
    kernel = functools.partial(update_kernel, parts, terms)
    return in_vmem(kernel, "update", [shape] * 3)(maps, first_moment, second_moment, *flat, *edge_grads)


def pairings(axis, ring):
    count = lax.axis_size(axis)
    first = [(i, i + 1) for i in range(0, count - 1, 2)]
    second = [(i, i + 1) for i in range(1, count - 1, 2)]
    if ring and count % 2 == 0 and count > 2:
        second.append((0, count - 1))
    return [swaps + [(target, source) for source, target in swaps] for swaps in (first, second)]


def swapped(arrays, axis, ring):
    return [lax.ppermute(array, axis, swaps) for array, swaps in zip(arrays, pairings(axis, ring))]


def both_scenarios(value):
    count = lax.axis_size("scen")
    if count == 2:
        return [value, lax.ppermute(value, "scen", [(0, 1), (1, 0)])]
    return [lax.psum(value, "scen")]


def shards(
    density,
    trait,
    variance,
    optimum,
    observed,
    obs_step,
    land_code,
    maps,
    first_moment,
    second_moment,
):
    sources = (density, trait, variance, optimum, observed, land_code, maps)
    rows = maps.shape[1]
    upper, fields, steps, *own_sides = first_window(CUTS[0] + EDGE, CUTS[0], sources, obs_step)
    upper_terms = both_scenarios(upper)
    sides = swapped(own_sides, "ly", RINGS[1])
    middle = window(CUTS[0] - HALO, CUTS[1] - CUTS[0] + EDGE, CUTS[0], CUTS[1] - CUTS[0], fields, steps, *own_sides)
    middle_terms = both_scenarios(middle)
    own_ends = pack_rows(fields, steps, *sides)
    ends = swapped(own_ends, "lx", RINGS[0])
    last = rows - CUTS[1]
    after = *own_sides, *sides, *own_ends, upper_terms[-1]
    lower = window(CUTS[1] - EDGE, last + EDGE, CUTS[1], last, fields, steps, *after)
    lower_terms = both_scenarios(lower)
    outer = edges(fields, steps, *own_sides, *sides, *ends)
    outer_terms = both_scenarios(outer)
    return tuple(update(maps, first_moment, second_moment, [upper_terms, middle_terms, lower_terms], outer_terms))


def solution(mesh):
    in_specs = (
        P("scen", "lx", "ly"),
        P("scen", "lx", "ly"),
        P("scen", "lx", "ly"),
        P("scen", "lx", "ly"),
        P("scen", "lx", "ly"),
        P("scen", "lx"),
        P("lx", "ly"),
        P(None, "lx", "ly"),
        P(None, "lx", "ly"),
        P(None, "lx", "ly"),
    )
    out_specs = (P(None, "lx", "ly"), P(None, "lx", "ly"), P(None, "lx", "ly"))
    return jax.shard_map(shards, mesh=mesh, in_specs=in_specs, out_specs=out_specs, check_vma=False)
```

```python
import functools
import math

import jax
import jax.numpy as jnp
from jax import lax
from jax.experimental import pallas as pl
from jax.experimental.pallas import tpu as pltpu
from jax.sharding import PartitionSpec as P

STEPS = 2
ADAM_STEP = 10
REACH_MAX = 0.2
PRIOR_WEIGHT = 0.1
GROWTH_RATE = 0.5
MUTATION_INPUT = 0.02
LEARN_RATE = 0.01
BETA_FIRST = 0.9
BETA_SECOND = 0.999
ADAM_EPS = 1e-08
LOSS_WEIGHT = 2.0

LOG2_E = math.log2(math.e)
HALF_LN_2 = 0.5 * math.log(2.0)

F32 = jnp.float32
LANES = 128
EDGE = 8
HALO = 4
DENSITY, TRAIT, VARIANCE, DISPERSAL, SELECTION, OPTIMUM, LAND, OBSERVED = range(8)
FIELDS = 8
ENDS_MEET = {"lx": True, "ly": False}
GROUPS = {5: (5, 5, 5, 5, 5, 5), 9: (9, 9, 3, 3, 3, 9), 10: (10, 10, 5, 5, 5, 10), 8: (8, 8, 4, 4, 4, 8), 12: (12, 12, 6, 6, 6, 12)}
CUTS = (32, 96)
WINDOW_US, EDGES_US = 4, 20
VMEM_BYTES = 16 * 1024 * 1024
SAVED = (
    "half",
    "land",
    "rate",
    "hs",
    "n0",
    "z0",
    "u0",
    "q0",
    "m0",
    "ld",
    "wd",
    "wr",
    "lr",
    "dr0n",
    "dr0q",
    "dr0m",
    "e",
    "d",
    "vs",
    "p",
    "zs",
    "es",
    "misfit",
    "r",
    "n1",
    "q1",
    "m1",
    "z1",
    "u1",
    "dr1n",
    "dr1q",
    "dr1m",
    "a2n",
    "a2q",
    "a2m",
    "gsel",
    "gd",
    "gr",
    "a1n",
    "a1q",
    "a1m",
)


def cost(microseconds):
    return pl.CostEstimate(flops=int(microseconds * 1e9), transcendentals=0, bytes_accessed=int(microseconds * 3.6e6))


def reciprocal(value):
    return 1.0 / value


def dynamics(slabs, groups, cycles, load, steps_at, keep, put):
    lane = lax.broadcasted_iota(jnp.int32, (sum(cycles), 8, LANES), 2)
    at_last, at_first = lane == LANES - 1, lane == 0

    def turn_tiles(value, by):
        parts, start = [], 0
        for count in cycles:
            cut = start + by % count
            parts += [value[cut : start + count], value[start:cut]]
            start += count
        return jnp.concatenate([part for part in parts if part.shape[0]], 0)

    def right(value):
        turned = pltpu.roll(value, LANES - 1, 2)
        return jnp.where(at_last, turn_tiles(turned, 1), turned)

    def left(value):
        turned = pltpu.roll(value, 1, 2)
        return jnp.where(at_first, turn_tiles(turned, -1), turned)

    def each_slab(stage, body, carry=()):
        group = groups[stage]

        def step(index, carry):
            held = {}

            def reader(offset):
                def at(name, ahead=0, tile=None):
                    if tile is not None:
                        return keep[name][index * group + offset, tile]
                    place = name, offset + ahead
                    if place not in held:
                        held[place] = keep[name][index * group + offset + ahead]
                    return held[place]

                return at

            for offset in range(group):
                carry = body(index * group + offset, reader(offset), carry)
            return carry

        if group == slabs:
            return step(0, carry)
        return lax.fori_loop(0, slabs // group, step, carry)

    def last(name, ahead=0):
        return keep[name][slabs - 1 + ahead]

    def close(names):
        for name in names:
            keep[name][slabs] = pltpu.roll(keep[name][0], 7, 1)

    def wrapped(values):
        return tuple(pltpu.roll(value, 1, 1) for value in values)

    def down_gap(name, at):
        return at(name, 1) - at(name)

    def row_fluxes(names, at):
        weight = at("wd")
        gaps = [down_gap(name, at) for name in names]
        return gaps, tuple(weight * gap for gap in gaps)

    def spread(names, at, above):
        row_gaps, row_flux = row_fluxes(names, at)
        weight = at("wr")
        out, col_gaps = [], []
        for name, flux, before in zip(names, row_flux, above):
            value = at(name)
            gap = right(value) - value
            col_flux = weight * gap
            out.append(value + (flux - before) + (col_flux - left(col_flux)))
            col_gaps.append(gap)
        return out, row_gaps, col_gaps, row_flux

    def begin(k, at, _):
        for t in range(sum(cycles)):
            keep["half"][k, t] = 0.25 * REACH_MAX + 0.25 * REACH_MAX * jnp.tanh(0.5 * load(DISPERSAL, k, t))
            land = load(LAND, k, t)
            keep["land"][k, t] = land
            keep["rate"][k, t] = LOG2_E * land
            raw = load(SELECTION, k, t)
            keep["hs"][k, t] = 0.5 * jnp.maximum(raw, 0.0) + HALF_LN_2 * jnp.log2(1.0 + jnp.exp2(-LOG2_E * jnp.abs(raw)))
            n, z, v = load(DENSITY, k, t), load(TRAIT, k, t), load(VARIANCE, k, t)
            u = v + z * z
            keep["n0"][k, t] = n
            keep["z0"][k, t] = z
            keep["u0"][k, t] = u
            keep["q0"][k, t] = n * z
            keep["m0"][k, t] = n * u
        return ()

    each_slab(0, begin)
    close(("half", "land", "n0", "q0", "m0"))

    def weigh(k, at, _):
        half, land = at("half"), at("land")
        pair = land * at("land", 1)
        keep["ld"][k] = pair
        keep["wd"][k] = (half + at("half", 1)) * pair
        pair = land * right(land)
        keep["lr"][k] = pair
        keep["wr"][k] = (half + right(half)) * pair
        return ()

    each_slab(1, weigh)
    first_names, second_names = ("n0", "q0", "m0"), ("n1", "q1", "m1")

    def first_step(k, at, above):
        spreads, _, col_gaps, above = spread(first_names, at, above)
        for name, gap in zip(("dr0n", "dr0q", "dr0m"), col_gaps):
            keep[name][k] = gap
        for t in range(sum(cycles)):
            ns, qs, ms = (value[t] for value in spreads)
            optimum, hs = load(OPTIMUM, k, t), at("hs", tile=t)
            r = reciprocal(ns + PRIOR_WEIGHT)
            zs = (qs + PRIOR_WEIGHT * at("z0", tile=t)) * r
            es = (ms + PRIOR_WEIGHT * at("u0", tile=t)) * r
            vs = es - zs * zs
            d = zs - optimum
            misfit = d * d + vs
            p = reciprocal(1.0 + (hs + hs) * vs)
            e = jnp.exp2(at("rate", tile=t) * (GROWTH_RATE - GROWTH_RATE * ns - hs * misfit))
            n1 = ns * e
            z1 = optimum + p * d
            u1 = vs * p + MUTATION_INPUT + z1 * z1
            for name, value in zip(
                ("e", "d", "vs", "p", "zs", "es", "misfit", "r", "n1", "q1", "m1", "z1", "u1"),
                (e, d, vs, p, zs, es, misfit, r, n1, n1 * z1, n1 * u1, z1, u1),
            ):
                keep[name][k, t] = value
        return above

    each_slab(2, first_step, wrapped(row_fluxes(first_names, last)[1]))
    close(second_names)

    def second_step(k, at, above):
        spreads, _, col_gaps, above = spread(second_names, at, above)
        for name, gap in zip(("dr1n", "dr1q", "dr1m"), col_gaps):
            keep[name][k] = gap
        for t in range(sum(cycles)):
            ns, qs, ms = (value[t] for value in spreads)
            optimum, hs, land = load(OPTIMUM, k, t), at("hs", tile=t), at("land", tile=t)
            r = reciprocal(ns + PRIOR_WEIGHT)
            zs = (qs + PRIOR_WEIGHT * at("z1", tile=t)) * r
            es = (ms + PRIOR_WEIGHT * at("u1", tile=t)) * r
            vs = es - zs * zs
            d = zs - optimum
            misfit = d * d + vs
            e = jnp.exp2(at("rate", tile=t) * (GROWTH_RATE - GROWTH_RATE * ns - hs * misfit))
            n2 = ns * e
            an = jnp.where(steps_at(k, t) == 2.0, land, 0.0) * (n2 - load(OBSERVED, k, t))
            b = an * n2
            am = -(b * hs) * r
            aq = (-2.0 * optimum) * am
            keep["gsel"][k, t] = b * misfit
            keep["a2n"][k, t] = an * e - 0.5 * b - (aq * zs + am * es)
            keep["a2q"][k, t] = aq
            keep["a2m"][k, t] = am
        return above

    each_slab(3, second_step, wrapped(row_fluxes(second_names, last)[1]))
    second_back, first_back = ("a2n", "a2q", "a2m"), ("a1n", "a1q", "a1m")
    close(second_back)

    def back(k, at, above):
        spreads, row_gaps, col_gaps, above = spread(second_back, at, above)
        n_gap, q_gap, m_gap = [down_gap(name, at) * gap for name, gap in zip(second_names, row_gaps)]
        keep["gd"][k] = n_gap + q_gap + m_gap
        n_gap, q_gap, m_gap = [at(f) * gap for f, gap in zip(("dr1n", "dr1q", "dr1m"), col_gaps)]
        keep["gr"][k] = n_gap + q_gap + m_gap
        for t in range(sum(cycles)):
            an, aq, am = (value[t] for value in spreads)
            n1, z1, land, hs = at("n1", tile=t), at("z1", tile=t), at("land", tile=t), at("hs", tile=t)
            e, d, vs, p, zs, es, r = (at(name, tile=t) for name in ("e", "d", "vs", "p", "zs", "es", "r"))
            av = PRIOR_WEIGHT * at("a2m", tile=t) + am * n1
            az = PRIOR_WEIGHT * at("a2q", tile=t) + aq * n1 + (z1 + z1) * av
            an = an + aq * z1 + am * at("u1", tile=t) + jnp.where(steps_at(k, t) == 1.0, land, 0.0) * (n1 - load(OBSERVED, k, t))
            b = an * n1 * land
            bs = b * hs
            ar = (az * d + av * vs) * ((p + p) * p)
            gsel = at("gsel", tile=t) + ar * vs + b * at("misfit", tile=t)
            avs = av * p - ar * hs - bs
            azs = az * p - 2.0 * (bs * d + zs * avs)
            aqs, ams = azs * r, avs * r
            keep["a1n"][k, t] = an * e - 0.5 * b - (aqs * zs + ams * es)
            keep["a1q"][k, t] = aqs
            keep["a1m"][k, t] = ams
            raw = load(SELECTION, k, t)
            put(1, k, t, gsel * (-0.5 * LOSS_WEIGHT - 0.5 * LOSS_WEIGHT * jnp.tanh(0.5 * raw)))
        return above

    each_slab(4, back, wrapped(row_fluxes(second_back, last)[1]))
    close(first_back)

    def row_share(at):
        n_gap, q_gap, m_gap = [down_gap(a, at) * down_gap(f, at) for a, f in zip(first_back, first_names)]
        return (at("gd") + n_gap + q_gap + m_gap) * at("ld")

    def finish(k, at, above):
        here = row_share(at)
        total = at("gr")
        for name, field in zip(first_back, ("dr0n", "dr0q", "dr0m")):
            value = at(name)
            total = total + (right(value) - value) * at(field)
        total = total * at("lr")
        half = at("half")
        scale = half * (2.0 * LOSS_WEIGHT / (0.5 * REACH_MAX) * half - 2.0 * LOSS_WEIGHT)
        total = scale * (here + above[0] + total + left(total))
        for t in range(sum(cycles)):
            put(0, k, t, total[t])
        return (here,)

    each_slab(5, finish, wrapped((row_share(last),)))


def step_rows(line):
    return jnp.transpose(jnp.concatenate([line] * (LANES // 8), 0))


def tile_copies(tiles, first, rows, sources, fields, codes, sems):
    density, trait, variance, optimum, observed, land_code, maps = sources
    moves = (
        (maps, fields.at[DISPERSAL : SELECTION + 1]),
        (land_code, codes),
        (density.at[0], fields.at[DENSITY]),
        (trait.at[0], fields.at[TRAIT]),
        (variance.at[0], fields.at[VARIANCE]),
        (optimum.at[0], fields.at[OPTIMUM]),
        (observed.at[0], fields.at[OBSERVED]),
    )
    part = pl.ds(first, rows)
    copies = []
    for index, (source, target) in enumerate(moves):
        for t in range(tiles):
            lanes = pl.ds(t * LANES, LANES)
            if source is maps:
                ends = source.at[:, part, lanes], target.at[:, t, part]
            else:
                ends = source.at[part, lanes], target.at[t, part]
            copies.append(pltpu.make_async_copy(*ends, sems.at[index, t]))
    return copies


def window_kernel(first, rows, skip, fields, steps, *refs):
    out_ref, grads, kept = refs[-3:]
    tiles = fields.shape[1]
    out_rows = out_ref.shape[1]
    slabs = rows // 8

    def load(field, k, t):
        return fields[field, t, pl.ds(first + k, 8, stride=slabs), :]

    def steps_at(k, t):
        return steps[0, pl.ds(first + k, 8, stride=slabs), :]

    def put(which, k, t, value):
        grads[which, t, pl.ds(k, 8, stride=slabs), :] = value

    keep = {name: kept.at[index] for index, name in enumerate(SAVED)}
    dynamics(slabs, GROUPS[slabs], (tiles,), load, steps_at, keep, put)
    for which in range(2):
        for t in range(tiles):
            out_ref[which, :, t * LANES : (t + 1) * LANES] = grads[which, t, skip : skip + out_rows, :]


def first_kernel(tiles, rows, *refs):
    sources, step_ref = refs[:7], refs[7]
    out_ref, fields, steps, pair_ref, other_ref, codes, line, grads, kept, sems, late_sems = refs[8:]
    height = fields.shape[2]
    early = tile_copies(tiles, 0, rows, sources, fields, codes, sems)
    late = tile_copies(tiles, rows, height - rows, sources, fields, codes, late_sems)
    early.append(pltpu.make_async_copy(step_ref, line, sems.at[7, 0]))
    for copy in early + late:
        copy.start()
    for copy in early:
        copy.wait()
    fields[LAND, :, :rows] = codes[:, :rows].astype(F32)
    wide = jnp.broadcast_to(line[0:1, :].astype(F32), (8, LANES))
    steps[0] = step_rows(wide)
    steps[1] = jnp.broadcast_to(wide[0:1], (LANES, LANES))
    window_kernel(0, rows, 0, fields, steps, out_ref, grads, kept)
    for copy in late:
        copy.wait()
    fields[LAND, :, rows:] = codes[:, rows:].astype(F32)
    columns_kernel(fields, pair_ref, other_ref)


def first_window(rows, out_rows, sources, obs_step):
    height, columns = sources[0].shape[1:]
    tiles = columns // LANES
    strip = jax.ShapeDtypeStruct((FIELDS, EDGE, height), F32)
    return pl.pallas_call(
        functools.partial(first_kernel, tiles, rows),
        out_shape=[
            jax.ShapeDtypeStruct((2, out_rows, columns), F32),
            jax.ShapeDtypeStruct((FIELDS, tiles, height, LANES), F32),
            jax.ShapeDtypeStruct((2, LANES, LANES), F32),
            strip,
            strip,
        ],
        in_specs=[pl.BlockSpec(memory_space=pltpu.HBM)] * 8,
        out_specs=[pl.BlockSpec(memory_space=pltpu.VMEM)] * 5,
        scratch_shapes=[
            pltpu.VMEM((tiles, height, LANES), jnp.int32),
            pltpu.VMEM(obs_step.shape, jnp.int32),
            pltpu.VMEM((2, tiles, rows, LANES), F32),
            pltpu.VMEM((len(SAVED), rows // 8 + 1, tiles, 8, LANES), F32),
            pltpu.SemaphoreType.DMA((8, tiles)),
            pltpu.SemaphoreType.DMA((7, tiles)),
        ],
        cost_estimate=cost(WINDOW_US),
        compiler_params=pltpu.CompilerParams(vmem_limit_bytes=VMEM_BYTES),
        name="first_window",
    )(*(pltpu.with_memory_space_constraint(source, pltpu.HBM) for source in (*sources, obs_step)))


def window(first, rows, out_first, out_rows, fields, steps, *after):
    tiles = fields.shape[1]
    return pl.pallas_call(
        functools.partial(window_kernel, first, rows, out_first - first),
        out_shape=jax.ShapeDtypeStruct((2, out_rows, tiles * LANES), F32),
        in_specs=[pl.BlockSpec(memory_space=pltpu.VMEM)] * 2 + [pl.BlockSpec(memory_space=pltpu.VMEM)] * len(after),
        out_specs=pl.BlockSpec(memory_space=pltpu.VMEM),
        scratch_shapes=[
            pltpu.VMEM((2, tiles, rows, LANES), F32),
            pltpu.VMEM((len(SAVED), rows // 8 + 1, tiles, 8, LANES), F32),
        ],
        cost_estimate=cost(WINDOW_US),
        compiler_params=pltpu.CompilerParams(vmem_limit_bytes=VMEM_BYTES),
        name=f"window_{out_first}",
    )(fields, steps, *after)


def columns_kernel(fields, pair_ref, other_ref):
    rightward = is_even("ly")
    tiles, rows = fields.shape[1:3]
    lane = lax.broadcasted_iota(jnp.int32, (rows, LANES), 1)
    packed = jnp.zeros((rows, LANES), F32)
    for field in range(FIELDS):
        both = jnp.where(lane < EDGE, fields[field, 0], fields[field, tiles - 1])
        turned = pltpu.roll(both, 16 * field, 1) if field else both
        place = (lane - 16 * field + EDGE) % LANES
        packed = jnp.where(place < 2 * EDGE, turned, packed)
    flipped = jnp.transpose(packed)
    for field in range(FIELDS):
        left = flipped[16 * field : 16 * field + EDGE]
        start = (16 * field - EDGE) % LANES
        right = flipped[start : start + EDGE]
        pair_ref[field] = jnp.where(rightward, right, left)
        other_ref[field] = jnp.where(rightward, left, right)


def in_vmem(kernel, name, out_shape):
    def call(*operands):
        many = isinstance(out_shape, (list, tuple))
        space = pl.BlockSpec(memory_space=pltpu.VMEM)
        return pl.pallas_call(
            kernel,
            out_shape=out_shape,
            in_specs=[space] * len(operands),
            out_specs=[space] * len(out_shape) if many else space,
            compiler_params=pltpu.CompilerParams(vmem_limit_bytes=VMEM_BYTES),
            name=name,
        )(*operands)

    return call


def is_even(axis):
    return lax.axis_index(axis) % 2 == 0


def present(axis):
    place = lax.axis_index(axis)
    return (place > 0).astype(F32), (place < lax.axis_size(axis) - 1).astype(F32)


def chosen(which, one, other):
    return lambda index: jnp.where(which, one[index], other[index])


def rows_kernel(fields, steps, from_pair, from_other, pair_ref, other_ref):
    tiles = fields.shape[1]
    downward, rightward = is_even("lx"), is_even("ly")
    sub = lax.broadcasted_iota(jnp.int32, (8, LANES), 0)
    for pair in range(FIELDS // 2):
        for t in range(tiles):
            even, odd = fields.at[2 * pair, t], fields.at[2 * pair + 1, t]
            up = jnp.where(sub < HALO, even[:EDGE], pltpu.roll(odd[:EDGE], HALO, 0))
            down = jnp.where(sub < HALO, pltpu.roll(odd[-EDGE:], HALO, 0), even[-EDGE:])
            pair_ref[pair * tiles + t] = jnp.where(downward, down, up)
            other_ref[pair * tiles + t] = jnp.where(downward, up, down)
    lane = lax.broadcasted_iota(jnp.int32, (8, LANES), 1)
    base = FIELDS // 2 * tiles
    strips = chosen(rightward, from_other, from_pair), chosen(rightward, from_pair, from_other)
    for index, strip in enumerate(strips):
        packed = jnp.zeros((8, LANES), F32)
        for field in range(FIELDS):
            turned = pltpu.roll(strip(field), 8 * field, 1) if field else strip(field)
            place = (lane - 8 * field + HALO) % LANES
            packed = jnp.where(place < 2 * HALO, turned, packed)
        pair_ref[base + index] = packed
        other_ref[base + index] = packed
    pair_ref[base + 2] = steps[1, :8]
    other_ref[base + 2] = steps[1, :8]


def pack_rows(*operands):
    fields = operands[0]
    shape = jax.ShapeDtypeStruct((FIELDS // 2 * fields.shape[1] + 3, 8, LANES), F32)
    return in_vmem(rows_kernel, "pack_rows", [shape, shape])(*operands)


def outer_rows(grad, which, t):
    sub = lax.broadcasted_iota(jnp.int32, (8, LANES), 0)
    return jnp.where(sub < HALO, grad[which, t, 8:16, :], grad[which, t, 16:24, :])


def edges_kernel(fields, steps, own_pair, own_other, side_pair, side_other, end_pair, end_other, *refs):
    out_ref, strip, grad, kept, row_step = refs
    tiles = fields.shape[1]
    base = FIELDS // 2 * tiles
    (has_above, has_below), (has_left, has_right) = present("lx"), present("ly")
    downward, rightward = is_even("lx"), is_even("ly")
    own_left, own_right = chosen(rightward, own_other, own_pair), chosen(rightward, own_pair, own_other)
    from_left, from_right = chosen(rightward, side_other, side_pair), chosen(rightward, side_pair, side_other)
    from_above, from_below = chosen(downward, end_other, end_pair), chosen(downward, end_pair, end_other)
    lane = lax.broadcasted_iota(jnp.int32, (8, LANES), 1)
    sub = lax.broadcasted_iota(jnp.int32, (8, LANES), 0)
    within = jnp.where(lane < LANES // 2, has_below, has_above)

    def lined(value, outer):
        out = jnp.where(lane < 8, pltpu.roll(outer, 8, 1), pltpu.roll(value, 8, 1))
        out = jnp.where(lane < 16, out, pltpu.roll(value, 24, 1))
        return jnp.where(lane < 24, out, pltpu.roll(outer, 24, 1))

    def beside(side, index, present):
        corners = jnp.where((lane % 8) < HALO, from_below(base + index), from_above(base + index))
        out = []
        for field in range(FIELDS):
            value = side(field)
            outer = pltpu.roll(corners, (LANES - 8 * field) % LANES, 1) if field else corners
            if field == LAND:
                value, outer = value * present, outer * (within * present)
            out.append(lined(value, outer))
        return out

    lefts, rights = beside(from_left, 0, has_left), beside(from_right, 1, has_right)
    zeros = jnp.zeros((8, LANES), F32)
    stack = []
    for index in range(LANES // 8):
        following = (index + 1) % (LANES // 8)
        here = rights[index] if index < FIELDS else zeros
        after = lefts[following] if following < FIELDS else zeros
        stack.append(jnp.where(sub < HALO, here, after))
    flipped = jnp.transpose(jnp.concatenate(stack, 0))[:32]
    outer_step = jnp.where(lane < LANES // 2, from_below(base + 2), from_above(base + 2))
    row_step[...] = step_rows(lined(steps[1, :8], outer_step))[:32]
    for field in range(FIELDS):
        for t in range(tiles):
            above, below = from_above(field // 2 * tiles + t), from_below(field // 2 * tiles + t)
            if field % 2:
                above, below = pltpu.roll(above, HALO, 0), pltpu.roll(below, HALO, 0)
            if field == LAND:
                above, below = above * has_above, below * has_below
            own = fields.at[field, t]
            for index, value in enumerate((above, own[:EDGE], own[-EDGE:], below)):
                strip[field, t, 8 * index : 8 * index + 8, :] = value
        strip[field, tiles] = pltpu.roll(flipped, (LANES - 8 * field) % LANES, 1) if field else flipped
        left, right = from_left(field), from_right(field)
        if field == LAND:
            left, right = left * has_left, right * has_right
        for index, value in enumerate((left, own_left(field), own_right(field), right)):
            strip[field, tiles + 1, 8 * index : 8 * index + 8, :] = value

    slabs = 3
    count = tiles + 2

    def load(field, k, t):
        return strip[field, t, pl.ds(HALO + k, 8, stride=slabs), :]

    def steps_at(k, t):
        return row_step[pl.ds(HALO + k, 8, stride=slabs), :] if t <= tiles else steps[1, :8]

    def put(which, k, t, value):
        grad[which, t, pl.ds(HALO + k, 8, stride=slabs), :] = value

    keep = {name: kept.at[index] for index, name in enumerate(SAVED)}
    dynamics(slabs, (slabs,) * 6, (tiles + 1, 1), load, steps_at, keep, put)
    for which in range(2):
        for t in range(tiles):
            out_ref[which, :, t * LANES : (t + 1) * LANES] = outer_rows(grad, which, t)
        out_ref[which, :, tiles * LANES :] = outer_rows(grad, which, tiles + 1)


def edges(fields, steps, *strips):
    tiles = fields.shape[1]
    count = tiles + 2
    space = pl.BlockSpec(memory_space=pltpu.VMEM)
    operands = [fields, steps, *strips]
    return pl.pallas_call(
        edges_kernel,
        out_shape=jax.ShapeDtypeStruct((2, EDGE, (tiles + 1) * LANES), F32),
        in_specs=[space] * len(operands),
        out_specs=space,
        scratch_shapes=[
            pltpu.VMEM((FIELDS, count, 32, LANES), F32),
            pltpu.VMEM((2, count, 32, LANES), F32),
            pltpu.VMEM((len(SAVED), 4, count, 8, LANES), F32),
            pltpu.VMEM((32, LANES), F32),
        ],
        cost_estimate=cost(EDGES_US),
        compiler_params=pltpu.CompilerParams(vmem_limit_bytes=VMEM_BYTES),
        name="edges",
    )(*operands)


def update_kernel(parts, terms, maps_ref, first_ref, second_ref, *refs):
    grads, edge_refs = refs[: parts * terms], refs[parts * terms : (parts + 1) * terms]
    new_maps, new_first, new_second = refs[(parts + 1) * terms :]
    rows, columns = maps_ref.shape[1:]
    tiles = columns // LANES
    lane = lax.broadcasted_iota(jnp.int32, (rows, LANES), 1)
    sub = lax.broadcasted_iota(jnp.int32, (EDGE, LANES), 0)
    edge = sum(ref[...] for ref in edge_refs)
    strips = [edge[which, :, columns:] for which in range(2)]
    blank = jnp.zeros((LANES - 2 * EDGE, LANES), F32)
    flipped = jnp.transpose(jnp.concatenate([*strips, blank], 0))
    for which in range(2):
        for t in range(tiles):
            own = slice(t * LANES, (t + 1) * LANES)
            grad = jnp.concatenate(
                [sum(ref[which, :, own] for ref in grads[part * terms : (part + 1) * terms]) for part in range(parts)],
                0,
            )
            if t == 0:
                beside = pltpu.roll(flipped, LANES - EDGE * which, 1) if which else flipped
                grad = jnp.where(lane < HALO, beside, grad)
            if t == tiles - 1:
                beside = pltpu.roll(flipped, LANES - EDGE * (which + 1), 1)
                grad = jnp.where(lane >= LANES - HALO, beside, grad)
            outer = edge[which, :, own]
            grad = jnp.concatenate(
                [
                    jnp.where(sub < HALO, outer, grad[:EDGE]),
                    grad[EDGE:-EDGE],
                    jnp.where(sub < HALO, grad[-EDGE:], outer),
                ],
                0,
            )
            first = BETA_FIRST * first_ref[which, :, own] + (1.0 - BETA_FIRST) * grad
            second = BETA_SECOND * second_ref[which, :, own] + (1.0 - BETA_SECOND) * grad * grad
            new_first[which, :, own] = first
            new_second[which, :, own] = second
            scale = jnp.sqrt(second * (1.0 / (1.0 - BETA_SECOND**ADAM_STEP))) + ADAM_EPS
            change = (LEARN_RATE / (1.0 - BETA_FIRST**ADAM_STEP)) * first
            new_maps[which, :, own] = maps_ref[which, :, own] - change * reciprocal(scale)


def update(maps, first_moment, second_moment, grads, edge_grads):
    parts, terms = len(grads), len(edge_grads)
    flat = [term for grad in grads for term in grad]
    shape = jax.ShapeDtypeStruct(maps.shape, F32)
    kernel = functools.partial(update_kernel, parts, terms)
    return in_vmem(kernel, "update", [shape] * 3)(maps, first_moment, second_moment, *flat, *edge_grads)


def swapped(arrays, axis, other):
    count, beside, columns = lax.axis_size(axis), lax.axis_size(other), lax.axis_size("ly")
    out = []
    for array, start in zip(arrays, (0, 1)):
        swaps = [(i, i + 1) for i in range(start, count - 1, 2)]
        alone = sorted(set(range(count)) - {i for swap in swaps for i in swap})
        pairs = [((i, k), (j, k)) for i, j in swaps for k in range(beside)]
        if ENDS_MEET[axis] and len(alone) == 2:
            pairs += [((alone[0], k), (alone[1], k)) for k in range(beside)]
        else:
            pairs += [((i, k), (i, k + 1)) for i in alone for k in range(0, beside - 1, 2)]
        if axis == "ly":
            pairs = [tuple(place[::-1] for place in pair) for pair in pairs]
        flat = [tuple(row * columns + column for row, column in pair) for pair in pairs]
        out.append(lax.ppermute(array, ("lx", "ly"), flat + [pair[::-1] for pair in flat]))
    return out


def both_scenarios(value):
    count = lax.axis_size("scen")
    if count == 2:
        return [value, lax.ppermute(value, "scen", [(0, 1), (1, 0)])]
    return [lax.psum(value, "scen")]


def shards(
    density,
    trait,
    variance,
    optimum,
    observed,
    obs_step,
    land_code,
    maps,
    first_moment,
    second_moment,
):
    sources = (density, trait, variance, optimum, observed, land_code, maps)
    rows = maps.shape[1]
    upper, fields, steps, *own_sides = first_window(CUTS[0] + EDGE, CUTS[0], sources, obs_step)
    upper_terms = both_scenarios(upper)
    sides = swapped(own_sides, "ly", "lx")
    middle = window(CUTS[0] - EDGE, CUTS[1] - CUTS[0] + 2 * EDGE, CUTS[0], CUTS[1] - CUTS[0], fields, steps, *own_sides)
    middle_terms = both_scenarios(middle)
    own_ends = pack_rows(fields, steps, *sides)
    ends = swapped(own_ends, "lx", "ly")
    last = rows - CUTS[1]
    after = *own_sides, *sides, *own_ends, upper_terms[-1]
    lower = window(CUTS[1] - EDGE, last + EDGE, CUTS[1], last, fields, steps, *after)
    lower_terms = both_scenarios(lower)
    outer = edges(fields, steps, *own_sides, *sides, *ends)
    outer_terms = both_scenarios(outer)
    return tuple(update(maps, first_moment, second_moment, [upper_terms, middle_terms, lower_terms], outer_terms))


def solution(mesh):
    in_specs = (
        P("scen", "lx", "ly"),
        P("scen", "lx", "ly"),
        P("scen", "lx", "ly"),
        P("scen", "lx", "ly"),
        P("scen", "lx", "ly"),
        P("scen", "lx"),
        P("lx", "ly"),
        P(None, "lx", "ly"),
        P(None, "lx", "ly"),
        P(None, "lx", "ly"),
    )
    out_specs = (P(None, "lx", "ly"), P(None, "lx", "ly"), P(None, "lx", "ly"))
    return jax.shard_map(shards, mesh=mesh, in_specs=in_specs, out_specs=out_specs, check_vma=False)
```

```python
import functools
import math

import jax
import jax.numpy as jnp
from jax import lax
from jax.experimental import pallas as pl
from jax.experimental.pallas import tpu as pltpu
from jax.sharding import PartitionSpec as P

STEPS = 2
ADAM_STEP = 10
REACH_MAX = 0.2
PRIOR_WEIGHT = 0.1
GROWTH_RATE = 0.5
MUTATION_INPUT = 0.02
LEARN_RATE = 0.01
BETA_FIRST = 0.9
BETA_SECOND = 0.999
ADAM_EPS = 1e-08
LOSS_WEIGHT = 2.0

LOG2_E = math.log2(math.e)
HALF_LN_2 = 0.5 * math.log(2.0)

F32 = jnp.float32
LANES = 128
EDGE = 8
HALO = 4
DENSITY, TRAIT, VARIANCE, DISPERSAL, SELECTION, OPTIMUM, LAND, OBSERVED = range(8)
FIELDS = 8
ENDS_MEET = {"lx": True, "ly": False}
GROUPS = {
    3: (3, 3, 3, 3, 3, 3),
    4: (4, 4, 4, 4, 4, 4),
    5: (5, 5, 5, 5, 5, 5),
    6: (6, 6, 6, 6, 6, 6),
    7: (7, 7, 7, 7, 7, 7),
    8: (8, 8, 4, 4, 4, 8),
    9: (9, 9, 3, 3, 3, 9),
    10: (10, 10, 5, 5, 5, 10),
    12: (12, 12, 6, 6, 6, 12),
}
APART = (6, 7)
CUTS = (40, 112)
WINDOW_US, EDGES_US = 4, 20
VMEM_BYTES = 16 * 1024 * 1024
SAVED = (
    "half",
    "land",
    "rate",
    "hs",
    "n0",
    "z0",
    "u0",
    "q0",
    "m0",
    "ld",
    "wd",
    "wr",
    "lr",
    "dr0n",
    "dr0q",
    "dr0m",
    "e",
    "d",
    "vs",
    "p",
    "zs",
    "es",
    "misfit",
    "r",
    "n1",
    "q1",
    "m1",
    "z1",
    "u1",
    "dr1n",
    "dr1q",
    "dr1m",
    "a2n",
    "a2q",
    "a2m",
    "gsel",
    "gd",
    "gr",
    "a1n",
    "a1q",
    "a1m",
)


def cost(microseconds):
    return pl.CostEstimate(flops=int(microseconds * 1e9), transcendentals=0, bytes_accessed=int(microseconds * 3.6e6))


def reciprocal(value):
    return 1.0 / value


def dynamics(slabs, groups, cycles, load, steps_at, keep, put):
    apart = slabs in APART
    once = (lax.axis_index("lx") >= 0).astype(jnp.int32) if apart else 1
    lane = lax.broadcasted_iota(jnp.int32, (sum(cycles), 8, LANES), 2)
    at_last, at_first = lane == LANES - 1, lane == 0

    def turn_tiles(value, by):
        parts, start = [], 0
        for count in cycles:
            cut = start + by % count
            parts += [value[cut : start + count], value[start:cut]]
            start += count
        return jnp.concatenate([part for part in parts if part.shape[0]], 0)

    def right(value):
        turned = pltpu.roll(value, LANES - 1, 2)
        return jnp.where(at_last, turn_tiles(turned, 1), turned)

    def left(value):
        turned = pltpu.roll(value, 1, 2)
        return jnp.where(at_first, turn_tiles(turned, -1), turned)

    def each_slab(stage, body, carry=()):
        group = groups[stage]

        def step(index, carry):
            held = {}

            def reader(offset):
                def at(name, ahead=0, tile=None):
                    if tile is not None:
                        return keep[name][index * group + offset, tile]
                    place = name, offset + ahead
                    if place not in held:
                        held[place] = keep[name][index * group + offset + ahead]
                    return held[place]

                return at

            for offset in range(group):
                carry = body(index * group + offset, reader(offset), carry)
            return carry

        if not apart and group == slabs:
            return step(0, carry)
        return lax.fori_loop(0, slabs // group * once, step, carry)

    def last(name, ahead=0):
        return keep[name][slabs - 1 + ahead]

    def close(names):
        for name in names:
            keep[name][slabs] = pltpu.roll(keep[name][0], 7, 1)

    def wrapped(values):
        return tuple(pltpu.roll(value, 1, 1) for value in values)

    def down_gap(name, at):
        return at(name, 1) - at(name)

    def row_fluxes(names, at):
        weight = at("wd")
        gaps = [down_gap(name, at) for name in names]
        return gaps, tuple(weight * gap for gap in gaps)

    def spread(names, at, above):
        row_gaps, row_flux = row_fluxes(names, at)
        weight = at("wr")
        out, col_gaps = [], []
        for name, flux, before in zip(names, row_flux, above):
            value = at(name)
            gap = right(value) - value
            col_flux = weight * gap
            out.append(value + (flux - before) + (col_flux - left(col_flux)))
            col_gaps.append(gap)
        return out, row_gaps, col_gaps, row_flux

    def begin(k, at, _):
        for t in range(sum(cycles)):
            keep["half"][k, t] = 0.25 * REACH_MAX + 0.25 * REACH_MAX * jnp.tanh(0.5 * load(DISPERSAL, k, t))
            land = load(LAND, k, t)
            keep["land"][k, t] = land
            keep["rate"][k, t] = LOG2_E * land
            raw = load(SELECTION, k, t)
            keep["hs"][k, t] = 0.5 * jnp.maximum(raw, 0.0) + HALF_LN_2 * jnp.log2(1.0 + jnp.exp2(-LOG2_E * jnp.abs(raw)))
            n, z, v = load(DENSITY, k, t), load(TRAIT, k, t), load(VARIANCE, k, t)
            u = v + z * z
            keep["n0"][k, t] = n
            keep["z0"][k, t] = z
            keep["u0"][k, t] = u
            keep["q0"][k, t] = n * z
            keep["m0"][k, t] = n * u
        return ()

    each_slab(0, begin)
    close(("half", "land", "n0", "q0", "m0"))

    def weigh(k, at, _):
        half, land = at("half"), at("land")
        pair = land * at("land", 1)
        keep["ld"][k] = pair
        keep["wd"][k] = (half + at("half", 1)) * pair
        pair = land * right(land)
        keep["lr"][k] = pair
        keep["wr"][k] = (half + right(half)) * pair
        return ()

    each_slab(1, weigh)
    first_names, second_names = ("n0", "q0", "m0"), ("n1", "q1", "m1")

    def first_step(k, at, above):
        spreads, _, col_gaps, above = spread(first_names, at, above)
        for name, gap in zip(("dr0n", "dr0q", "dr0m"), col_gaps):
            keep[name][k] = gap
        for t in range(sum(cycles)):
            ns, qs, ms = (value[t] for value in spreads)
            optimum, hs = load(OPTIMUM, k, t), at("hs", tile=t)
            r = reciprocal(ns + PRIOR_WEIGHT)
            zs = (qs + PRIOR_WEIGHT * at("z0", tile=t)) * r
            es = (ms + PRIOR_WEIGHT * at("u0", tile=t)) * r
            vs = es - zs * zs
            d = zs - optimum
            misfit = d * d + vs
            p = reciprocal(1.0 + (hs + hs) * vs)
            e = jnp.exp2(at("rate", tile=t) * (GROWTH_RATE - GROWTH_RATE * ns - hs * misfit))
            n1 = ns * e
            z1 = optimum + p * d
            u1 = vs * p + MUTATION_INPUT + z1 * z1
            for name, value in zip(
                ("e", "d", "vs", "p", "zs", "es", "misfit", "r", "n1", "q1", "m1", "z1", "u1"),
                (e, d, vs, p, zs, es, misfit, r, n1, n1 * z1, n1 * u1, z1, u1),
            ):
                keep[name][k, t] = value
        return above

    each_slab(2, first_step, wrapped(row_fluxes(first_names, last)[1]))
    close(second_names)

    def second_step(k, at, above):
        spreads, _, col_gaps, above = spread(second_names, at, above)
        for name, gap in zip(("dr1n", "dr1q", "dr1m"), col_gaps):
            keep[name][k] = gap
        for t in range(sum(cycles)):
            ns, qs, ms = (value[t] for value in spreads)
            optimum, hs, land = load(OPTIMUM, k, t), at("hs", tile=t), at("land", tile=t)
            r = reciprocal(ns + PRIOR_WEIGHT)
            zs = (qs + PRIOR_WEIGHT * at("z1", tile=t)) * r
            es = (ms + PRIOR_WEIGHT * at("u1", tile=t)) * r
            vs = es - zs * zs
            d = zs - optimum
            misfit = d * d + vs
            e = jnp.exp2(at("rate", tile=t) * (GROWTH_RATE - GROWTH_RATE * ns - hs * misfit))
            n2 = ns * e
            an = jnp.where(steps_at(k, t) == 2.0, land, 0.0) * (n2 - load(OBSERVED, k, t))
            b = an * n2
            am = -(b * hs) * r
            aq = (-2.0 * optimum) * am
            keep["gsel"][k, t] = b * misfit
            keep["a2n"][k, t] = an * e - 0.5 * b - (aq * zs + am * es)
            keep["a2q"][k, t] = aq
            keep["a2m"][k, t] = am
        return above

    each_slab(3, second_step, wrapped(row_fluxes(second_names, last)[1]))
    second_back, first_back = ("a2n", "a2q", "a2m"), ("a1n", "a1q", "a1m")
    close(second_back)

    def back(k, at, above):
        spreads, row_gaps, col_gaps, above = spread(second_back, at, above)
        n_gap, q_gap, m_gap = [down_gap(name, at) * gap for name, gap in zip(second_names, row_gaps)]
        keep["gd"][k] = n_gap + q_gap + m_gap
        n_gap, q_gap, m_gap = [at(f) * gap for f, gap in zip(("dr1n", "dr1q", "dr1m"), col_gaps)]
        keep["gr"][k] = n_gap + q_gap + m_gap
        for t in range(sum(cycles)):
            an, aq, am = (value[t] for value in spreads)
            n1, z1, land, hs = at("n1", tile=t), at("z1", tile=t), at("land", tile=t), at("hs", tile=t)
            e, d, vs, p, zs, es, r = (at(name, tile=t) for name in ("e", "d", "vs", "p", "zs", "es", "r"))
            av = PRIOR_WEIGHT * at("a2m", tile=t) + am * n1
            az = PRIOR_WEIGHT * at("a2q", tile=t) + aq * n1 + (z1 + z1) * av
            an = an + aq * z1 + am * at("u1", tile=t) + jnp.where(steps_at(k, t) == 1.0, land, 0.0) * (n1 - load(OBSERVED, k, t))
            b = an * n1 * land
            bs = b * hs
            ar = (az * d + av * vs) * ((p + p) * p)
            gsel = at("gsel", tile=t) + ar * vs + b * at("misfit", tile=t)
            avs = av * p - ar * hs - bs
            azs = az * p - 2.0 * (bs * d + zs * avs)
            aqs, ams = azs * r, avs * r
            keep["a1n"][k, t] = an * e - 0.5 * b - (aqs * zs + ams * es)
            keep["a1q"][k, t] = aqs
            keep["a1m"][k, t] = ams
            raw = load(SELECTION, k, t)
            put(1, k, t, gsel * (-0.5 * LOSS_WEIGHT - 0.5 * LOSS_WEIGHT * jnp.tanh(0.5 * raw)))
        return above

    each_slab(4, back, wrapped(row_fluxes(second_back, last)[1]))
    close(first_back)

    def row_share(at):
        n_gap, q_gap, m_gap = [down_gap(a, at) * down_gap(f, at) for a, f in zip(first_back, first_names)]
        return (at("gd") + n_gap + q_gap + m_gap) * at("ld")

    def finish(k, at, above):
        here = row_share(at)
        total = at("gr")
        for name, field in zip(first_back, ("dr0n", "dr0q", "dr0m")):
            value = at(name)
            total = total + (right(value) - value) * at(field)
        total = total * at("lr")
        half = at("half")
        scale = half * (2.0 * LOSS_WEIGHT / (0.5 * REACH_MAX) * half - 2.0 * LOSS_WEIGHT)
        total = scale * (here + above[0] + total + left(total))
        for t in range(sum(cycles)):
            put(0, k, t, total[t])
        return (here,)

    each_slab(5, finish, wrapped((row_share(last),)))


def step_rows(line):
    return jnp.transpose(jnp.concatenate([line] * (LANES // 8), 0))


def tile_copies(tiles, first, rows, sources, fields, codes, sems):
    density, trait, variance, optimum, observed, land_code, maps = sources
    moves = (
        (maps, fields.at[DISPERSAL : SELECTION + 1]),
        (land_code, codes),
        (density.at[0], fields.at[DENSITY]),
        (trait.at[0], fields.at[TRAIT]),
        (variance.at[0], fields.at[VARIANCE]),
        (optimum.at[0], fields.at[OPTIMUM]),
        (observed.at[0], fields.at[OBSERVED]),
    )
    part = pl.ds(first, rows)
    copies = []
    for index, (source, target) in enumerate(moves):
        for t in range(tiles):
            lanes = pl.ds(t * LANES, LANES)
            if source is maps:
                ends = source.at[:, part, lanes], target.at[:, t, part]
            else:
                ends = source.at[part, lanes], target.at[t, part]
            copies.append(pltpu.make_async_copy(*ends, sems.at[index, t]))
    return copies


def window_kernel(first, rows, skip, fields, steps, *refs):
    out_ref, grads, kept = refs[-3:]
    tiles = fields.shape[1]
    out_rows = out_ref.shape[1]
    slabs = rows // 8

    def load(field, k, t):
        return fields[field, t, pl.ds(first + k, 8, stride=slabs), :]

    def steps_at(k, t):
        return steps[0, pl.ds(first + k, 8, stride=slabs), :]

    def put(which, k, t, value):
        grads[which, t, pl.ds(k, 8, stride=slabs), :] = value

    keep = {name: kept.at[index] for index, name in enumerate(SAVED)}
    dynamics(slabs, GROUPS[slabs], (tiles,), load, steps_at, keep, put)
    for which in range(2):
        for t in range(tiles):
            out_ref[which, :, t * LANES : (t + 1) * LANES] = grads[which, t, skip : skip + out_rows, :]


def first_kernel(tiles, rows, *refs):
    sources, step_ref = refs[:7], refs[7]
    out_ref, fields, steps, pair_ref, other_ref, codes, line, grads, kept, sems, late_sems = refs[8:]
    height = fields.shape[2]
    early = tile_copies(tiles, 0, rows, sources, fields, codes, sems)
    late = tile_copies(tiles, rows, height - rows, sources, fields, codes, late_sems)
    early.append(pltpu.make_async_copy(step_ref, line, sems.at[7, 0]))
    for copy in early + late:
        copy.start()
    for copy in early:
        copy.wait()
    fields[LAND, :, :rows] = codes[:, :rows].astype(F32)
    wide = jnp.broadcast_to(line[0:1, :].astype(F32), (8, LANES))
    steps[0] = step_rows(wide)
    steps[1] = jnp.broadcast_to(wide[0:1], (LANES, LANES))
    window_kernel(0, rows, 0, fields, steps, out_ref, grads, kept)
    for copy in late:
        copy.wait()
    fields[LAND, :, rows:] = codes[:, rows:].astype(F32)
    columns_kernel(fields, pair_ref, other_ref)


def first_window(rows, out_rows, sources, obs_step):
    height, columns = sources[0].shape[1:]
    tiles = columns // LANES
    strip = jax.ShapeDtypeStruct((FIELDS, EDGE, height), F32)
    return pl.pallas_call(
        functools.partial(first_kernel, tiles, rows),
        out_shape=[
            jax.ShapeDtypeStruct((2, out_rows, columns), F32),
            jax.ShapeDtypeStruct((FIELDS, tiles, height, LANES), F32),
            jax.ShapeDtypeStruct((2, LANES, LANES), F32),
            strip,
            strip,
        ],
        in_specs=[pl.BlockSpec(memory_space=pltpu.HBM)] * 8,
        out_specs=[pl.BlockSpec(memory_space=pltpu.VMEM)] * 5,
        scratch_shapes=[
            pltpu.VMEM((tiles, height, LANES), jnp.int32),
            pltpu.VMEM(obs_step.shape, jnp.int32),
            pltpu.VMEM((2, tiles, rows, LANES), F32),
            pltpu.VMEM((len(SAVED), rows // 8 + 1, tiles, 8, LANES), F32),
            pltpu.SemaphoreType.DMA((8, tiles)),
            pltpu.SemaphoreType.DMA((7, tiles)),
        ],
        cost_estimate=cost(WINDOW_US),
        compiler_params=pltpu.CompilerParams(vmem_limit_bytes=VMEM_BYTES),
        name="first_window",
    )(*(pltpu.with_memory_space_constraint(source, pltpu.HBM) for source in (*sources, obs_step)))


def window(first, rows, out_first, out_rows, fields, steps, *after):
    tiles = fields.shape[1]
    return pl.pallas_call(
        functools.partial(window_kernel, first, rows, out_first - first),
        out_shape=jax.ShapeDtypeStruct((2, out_rows, tiles * LANES), F32),
        in_specs=[pl.BlockSpec(memory_space=pltpu.VMEM)] * 2 + [pl.BlockSpec(memory_space=pltpu.VMEM)] * len(after),
        out_specs=pl.BlockSpec(memory_space=pltpu.VMEM),
        scratch_shapes=[
            pltpu.VMEM((2, tiles, rows, LANES), F32),
            pltpu.VMEM((len(SAVED), rows // 8 + 1, tiles, 8, LANES), F32),
        ],
        cost_estimate=cost(WINDOW_US),
        compiler_params=pltpu.CompilerParams(vmem_limit_bytes=VMEM_BYTES),
        name=f"window_{out_first}",
    )(fields, steps, *after)


def columns_kernel(fields, pair_ref, other_ref):
    rightward = is_even("ly")
    tiles, rows = fields.shape[1:3]
    lane = lax.broadcasted_iota(jnp.int32, (rows, LANES), 1)
    packed = jnp.zeros((rows, LANES), F32)
    for field in range(FIELDS):
        both = jnp.where(lane < EDGE, fields[field, 0], fields[field, tiles - 1])
        turned = pltpu.roll(both, 16 * field, 1) if field else both
        place = (lane - 16 * field + EDGE) % LANES
        packed = jnp.where(place < 2 * EDGE, turned, packed)
    flipped = jnp.transpose(packed)
    for field in range(FIELDS):
        left = flipped[16 * field : 16 * field + EDGE]
        start = (16 * field - EDGE) % LANES
        right = flipped[start : start + EDGE]
        pair_ref[field] = jnp.where(rightward, right, left)
        other_ref[field] = jnp.where(rightward, left, right)


def in_vmem(kernel, name, out_shape):
    def call(*operands):
        many = isinstance(out_shape, (list, tuple))
        space = pl.BlockSpec(memory_space=pltpu.VMEM)
        return pl.pallas_call(
            kernel,
            out_shape=out_shape,
            in_specs=[space] * len(operands),
            out_specs=[space] * len(out_shape) if many else space,
            compiler_params=pltpu.CompilerParams(vmem_limit_bytes=VMEM_BYTES),
            name=name,
        )(*operands)

    return call


def is_even(axis):
    return lax.axis_index(axis) % 2 == 0


def present(axis):
    place = lax.axis_index(axis)
    return (place > 0).astype(F32), (place < lax.axis_size(axis) - 1).astype(F32)


def chosen(which, one, other):
    return lambda index: jnp.where(which, one[index], other[index])


def rows_kernel(fields, steps, from_pair, from_other, pair_ref, other_ref):
    tiles = fields.shape[1]
    downward, rightward = is_even("lx"), is_even("ly")
    sub = lax.broadcasted_iota(jnp.int32, (8, LANES), 0)
    for pair in range(FIELDS // 2):
        for t in range(tiles):
            even, odd = fields.at[2 * pair, t], fields.at[2 * pair + 1, t]
            up = jnp.where(sub < HALO, even[:EDGE], pltpu.roll(odd[:EDGE], HALO, 0))
            down = jnp.where(sub < HALO, pltpu.roll(odd[-EDGE:], HALO, 0), even[-EDGE:])
            pair_ref[pair * tiles + t] = jnp.where(downward, down, up)
            other_ref[pair * tiles + t] = jnp.where(downward, up, down)
    lane = lax.broadcasted_iota(jnp.int32, (8, LANES), 1)
    base = FIELDS // 2 * tiles
    strips = chosen(rightward, from_other, from_pair), chosen(rightward, from_pair, from_other)
    for index, strip in enumerate(strips):
        packed = jnp.zeros((8, LANES), F32)
        for field in range(FIELDS):
            turned = pltpu.roll(strip(field), 8 * field, 1) if field else strip(field)
            place = (lane - 8 * field + HALO) % LANES
            packed = jnp.where(place < 2 * HALO, turned, packed)
        pair_ref[base + index] = packed
        other_ref[base + index] = packed
    pair_ref[base + 2] = steps[1, :8]
    other_ref[base + 2] = steps[1, :8]


def pack_rows(*operands):
    fields = operands[0]
    shape = jax.ShapeDtypeStruct((FIELDS // 2 * fields.shape[1] + 3, 8, LANES), F32)
    return in_vmem(rows_kernel, "pack_rows", [shape, shape])(*operands)


def outer_rows(grad, which, t):
    sub = lax.broadcasted_iota(jnp.int32, (8, LANES), 0)
    return jnp.where(sub < HALO, grad[which, t, 8:16, :], grad[which, t, 16:24, :])


def edges_kernel(fields, steps, own_pair, own_other, side_pair, side_other, end_pair, end_other, *refs):
    out_ref, strip, grad, kept, row_step = refs
    tiles = fields.shape[1]
    base = FIELDS // 2 * tiles
    (has_above, has_below), (has_left, has_right) = present("lx"), present("ly")
    downward, rightward = is_even("lx"), is_even("ly")
    own_left, own_right = chosen(rightward, own_other, own_pair), chosen(rightward, own_pair, own_other)
    from_left, from_right = chosen(rightward, side_other, side_pair), chosen(rightward, side_pair, side_other)
    from_above, from_below = chosen(downward, end_other, end_pair), chosen(downward, end_pair, end_other)
    lane = lax.broadcasted_iota(jnp.int32, (8, LANES), 1)
    sub = lax.broadcasted_iota(jnp.int32, (8, LANES), 0)
    within = jnp.where(lane < LANES // 2, has_below, has_above)

    def lined(value, outer):
        out = jnp.where(lane < 8, pltpu.roll(outer, 8, 1), pltpu.roll(value, 8, 1))
        out = jnp.where(lane < 16, out, pltpu.roll(value, 24, 1))
        return jnp.where(lane < 24, out, pltpu.roll(outer, 24, 1))

    def beside(side, index, present):
        corners = jnp.where((lane % 8) < HALO, from_below(base + index), from_above(base + index))
        out = []
        for field in range(FIELDS):
            value = side(field)
            outer = pltpu.roll(corners, (LANES - 8 * field) % LANES, 1) if field else corners
            if field == LAND:
                value, outer = value * present, outer * (within * present)
            out.append(lined(value, outer))
        return out

    lefts, rights = beside(from_left, 0, has_left), beside(from_right, 1, has_right)
    zeros = jnp.zeros((8, LANES), F32)
    stack = []
    for index in range(LANES // 8):
        following = (index + 1) % (LANES // 8)
        here = rights[index] if index < FIELDS else zeros
        after = lefts[following] if following < FIELDS else zeros
        stack.append(jnp.where(sub < HALO, here, after))
    flipped = jnp.transpose(jnp.concatenate(stack, 0))[:32]
    outer_step = jnp.where(lane < LANES // 2, from_below(base + 2), from_above(base + 2))
    row_step[...] = step_rows(lined(steps[1, :8], outer_step))[:32]
    for field in range(FIELDS):
        for t in range(tiles):
            above, below = from_above(field // 2 * tiles + t), from_below(field // 2 * tiles + t)
            if field % 2:
                above, below = pltpu.roll(above, HALO, 0), pltpu.roll(below, HALO, 0)
            if field == LAND:
                above, below = above * has_above, below * has_below
            own = fields.at[field, t]
            for index, value in enumerate((above, own[:EDGE], own[-EDGE:], below)):
                strip[field, t, 8 * index : 8 * index + 8, :] = value
        strip[field, tiles] = pltpu.roll(flipped, (LANES - 8 * field) % LANES, 1) if field else flipped
        left, right = from_left(field), from_right(field)
        if field == LAND:
            left, right = left * has_left, right * has_right
        for index, value in enumerate((left, own_left(field), own_right(field), right)):
            strip[field, tiles + 1, 8 * index : 8 * index + 8, :] = value

    slabs = 3
    count = tiles + 2

    def load(field, k, t):
        return strip[field, t, pl.ds(HALO + k, 8, stride=slabs), :]

    def steps_at(k, t):
        return row_step[pl.ds(HALO + k, 8, stride=slabs), :] if t <= tiles else steps[1, :8]

    def put(which, k, t, value):
        grad[which, t, pl.ds(HALO + k, 8, stride=slabs), :] = value

    keep = {name: kept.at[index] for index, name in enumerate(SAVED)}
    dynamics(slabs, (slabs,) * 6, (tiles + 1, 1), load, steps_at, keep, put)
    for which in range(2):
        for t in range(tiles):
            out_ref[which, :, t * LANES : (t + 1) * LANES] = outer_rows(grad, which, t)
        out_ref[which, :, tiles * LANES :] = outer_rows(grad, which, tiles + 1)


def edges(fields, steps, *strips):
    tiles = fields.shape[1]
    count = tiles + 2
    space = pl.BlockSpec(memory_space=pltpu.VMEM)
    operands = [fields, steps, *strips]
    return pl.pallas_call(
        edges_kernel,
        out_shape=jax.ShapeDtypeStruct((2, EDGE, (tiles + 1) * LANES), F32),
        in_specs=[space] * len(operands),
        out_specs=space,
        scratch_shapes=[
            pltpu.VMEM((FIELDS, count, 32, LANES), F32),
            pltpu.VMEM((2, count, 32, LANES), F32),
            pltpu.VMEM((len(SAVED), 4, count, 8, LANES), F32),
            pltpu.VMEM((32, LANES), F32),
        ],
        cost_estimate=cost(EDGES_US),
        compiler_params=pltpu.CompilerParams(vmem_limit_bytes=VMEM_BYTES),
        name="edges",
    )(*operands)


def update_kernel(parts, terms, maps_ref, first_ref, second_ref, *refs):
    grads, edge_refs = refs[: parts * terms], refs[parts * terms : (parts + 1) * terms]
    new_maps, new_first, new_second = refs[(parts + 1) * terms :]
    rows, columns = maps_ref.shape[1:]
    tiles = columns // LANES
    lane = lax.broadcasted_iota(jnp.int32, (rows, LANES), 1)
    sub = lax.broadcasted_iota(jnp.int32, (EDGE, LANES), 0)
    edge = sum(ref[...] for ref in edge_refs)
    strips = [edge[which, :, columns:] for which in range(2)]
    blank = jnp.zeros((LANES - 2 * EDGE, LANES), F32)
    flipped = jnp.transpose(jnp.concatenate([*strips, blank], 0))
    for which in range(2):
        for t in range(tiles):
            own = slice(t * LANES, (t + 1) * LANES)
            grad = jnp.concatenate(
                [sum(ref[which, :, own] for ref in grads[part * terms : (part + 1) * terms]) for part in range(parts)],
                0,
            )
            if t == 0:
                beside = pltpu.roll(flipped, LANES - EDGE * which, 1) if which else flipped
                grad = jnp.where(lane < HALO, beside, grad)
            if t == tiles - 1:
                beside = pltpu.roll(flipped, LANES - EDGE * (which + 1), 1)
                grad = jnp.where(lane >= LANES - HALO, beside, grad)
            outer = edge[which, :, own]
            grad = jnp.concatenate(
                [
                    jnp.where(sub < HALO, outer, grad[:EDGE]),
                    grad[EDGE:-EDGE],
                    jnp.where(sub < HALO, grad[-EDGE:], outer),
                ],
                0,
            )
            first = BETA_FIRST * first_ref[which, :, own] + (1.0 - BETA_FIRST) * grad
            second = BETA_SECOND * second_ref[which, :, own] + (1.0 - BETA_SECOND) * grad * grad
            new_first[which, :, own] = first
            new_second[which, :, own] = second
            scale = jnp.sqrt(second * (1.0 / (1.0 - BETA_SECOND**ADAM_STEP))) + ADAM_EPS
            change = (LEARN_RATE / (1.0 - BETA_FIRST**ADAM_STEP)) * first
            new_maps[which, :, own] = maps_ref[which, :, own] - change * reciprocal(scale)


def update(maps, first_moment, second_moment, grads, edge_grads):
    parts, terms = len(grads), len(edge_grads)
    flat = [term for grad in grads for term in grad]
    shape = jax.ShapeDtypeStruct(maps.shape, F32)
    kernel = functools.partial(update_kernel, parts, terms)
    return in_vmem(kernel, "update", [shape] * 3)(maps, first_moment, second_moment, *flat, *edge_grads)


def swapped(arrays, axis, other):
    count, beside, columns = lax.axis_size(axis), lax.axis_size(other), lax.axis_size("ly")
    out = []
    for array, start in zip(arrays, (0, 1)):
        swaps = [(i, i + 1) for i in range(start, count - 1, 2)]
        alone = sorted(set(range(count)) - {i for swap in swaps for i in swap})
        pairs = [((i, k), (j, k)) for i, j in swaps for k in range(beside)]
        if ENDS_MEET[axis] and len(alone) == 2:
            pairs += [((alone[0], k), (alone[1], k)) for k in range(beside)]
        else:
            pairs += [((i, k), (i, k + 1)) for i in alone for k in range(0, beside - 1, 2)]
        if axis == "ly":
            pairs = [tuple(place[::-1] for place in pair) for pair in pairs]
        flat = [tuple(row * columns + column for row, column in pair) for pair in pairs]
        out.append(lax.ppermute(array, ("lx", "ly"), flat + [pair[::-1] for pair in flat]))
    return out


def both_scenarios(value):
    count = lax.axis_size("scen")
    if count == 2:
        return [value, lax.ppermute(value, "scen", [(0, 1), (1, 0)])]
    return [lax.psum(value, "scen")]


def shards(
    density,
    trait,
    variance,
    optimum,
    observed,
    obs_step,
    land_code,
    maps,
    first_moment,
    second_moment,
):
    sources = (density, trait, variance, optimum, observed, land_code, maps)
    rows = maps.shape[1]
    upper, fields, steps, *own_sides = first_window(CUTS[0] + EDGE, CUTS[0], sources, obs_step)
    upper_terms = both_scenarios(upper)
    sides = swapped(own_sides, "ly", "lx")
    middle = window(CUTS[0] - HALO, CUTS[1] - CUTS[0] + EDGE, CUTS[0], CUTS[1] - CUTS[0], fields, steps, *own_sides)
    middle_terms = both_scenarios(middle)
    own_ends = pack_rows(fields, steps, *sides)
    ends = swapped(own_ends, "lx", "ly")
    last = rows - CUTS[1]
    after = *own_sides, *sides, *own_ends, upper_terms[-1]
    lower = window(CUTS[1] - EDGE, last + EDGE, CUTS[1], last, fields, steps, *after)
    lower_terms = both_scenarios(lower)
    outer = edges(fields, steps, *own_sides, *sides, *ends)
    outer_terms = both_scenarios(outer)
    return tuple(update(maps, first_moment, second_moment, [upper_terms, middle_terms, lower_terms], outer_terms))


def solution(mesh):
    in_specs = (
        P("scen", "lx", "ly"),
        P("scen", "lx", "ly"),
        P("scen", "lx", "ly"),
        P("scen", "lx", "ly"),
        P("scen", "lx", "ly"),
        P("scen", "lx"),
        P("lx", "ly"),
        P(None, "lx", "ly"),
        P(None, "lx", "ly"),
        P(None, "lx", "ly"),
    )
    out_specs = (P(None, "lx", "ly"), P(None, "lx", "ly"), P(None, "lx", "ly"))
    return jax.shard_map(shards, mesh=mesh, in_specs=in_specs, out_specs=out_specs, check_vma=False)
```

```python
import functools
import math

import jax
import jax.numpy as jnp
from jax import lax
from jax.experimental import pallas as pl
from jax.experimental.pallas import tpu as pltpu
from jax.sharding import PartitionSpec as P

STEPS = 2
ADAM_STEP = 10
REACH_MAX = 0.2
PRIOR_WEIGHT = 0.1
GROWTH_RATE = 0.5
MUTATION_INPUT = 0.02
LEARN_RATE = 0.01
BETA_FIRST = 0.9
BETA_SECOND = 0.999
ADAM_EPS = 1e-08
LOSS_WEIGHT = 2.0

LOG2_E = math.log2(math.e)
HALF_LN_2 = 0.5 * math.log(2.0)

F32 = jnp.float32
LANES = 128
EDGE = 8
HALO = 4
DENSITY, TRAIT, VARIANCE, DISPERSAL, SELECTION, OPTIMUM, LAND, OBSERVED = range(8)
FIELDS = 8
ENDS_MEET = {"lx": True, "ly": False}
GROUPS = {
    3: (3, 3, 3, 3, 3, 3),
    4: (4, 4, 4, 4, 4, 4),
    5: (5, 5, 5, 5, 5, 5),
    6: (6, 6, 6, 6, 6, 6),
    7: (7, 7, 7, 7, 7, 7),
    8: (8, 8, 4, 4, 4, 8),
    9: (9, 9, 3, 3, 3, 9),
    10: (10, 10, 5, 5, 5, 10),
    12: (12, 12, 6, 6, 6, 12),
}
APART = (6, 7)
CUTS = (40, 112)
WINDOW_US, EDGES_US = 4, 20
VMEM_BYTES = 16 * 1024 * 1024
SAVED = (
    "half",
    "land",
    "rate",
    "hs",
    "n0",
    "z0",
    "u0",
    "q0",
    "m0",
    "ld",
    "wd",
    "wr",
    "lr",
    "dr0n",
    "dr0q",
    "dr0m",
    "e",
    "d",
    "vs",
    "p",
    "zs",
    "es",
    "misfit",
    "r",
    "n1",
    "q1",
    "m1",
    "z1",
    "u1",
    "dr1n",
    "dr1q",
    "dr1m",
    "a2n",
    "a2q",
    "a2m",
    "gsel",
    "gd",
    "gr",
    "a1n",
    "a1q",
    "a1m",
)


def cost(microseconds):
    return pl.CostEstimate(flops=int(microseconds * 1e9), transcendentals=0, bytes_accessed=int(microseconds * 3.6e6))


def reciprocal(value):
    return 1.0 / value


def dynamics(slabs, groups, cycles, load, steps_at, keep, put):
    apart = slabs in APART
    once = (lax.axis_index("lx") >= 0).astype(jnp.int32) if apart else 1
    lane = lax.broadcasted_iota(jnp.int32, (sum(cycles), 8, LANES), 2)
    at_last, at_first = lane == LANES - 1, lane == 0

    def turn_tiles(value, by):
        parts, start = [], 0
        for count in cycles:
            cut = start + by % count
            parts += [value[cut : start + count], value[start:cut]]
            start += count
        return jnp.concatenate([part for part in parts if part.shape[0]], 0)

    def right(value):
        turned = pltpu.roll(value, LANES - 1, 2)
        return jnp.where(at_last, turn_tiles(turned, 1), turned)

    def left(value):
        turned = pltpu.roll(value, 1, 2)
        return jnp.where(at_first, turn_tiles(turned, -1), turned)

    def each_slab(stage, body, carry=()):
        group = groups[stage]

        def step(index, carry):
            held = {}

            def reader(offset):
                def at(name, ahead=0, tile=None):
                    if tile is not None:
                        return keep[name][index * group + offset, tile]
                    place = name, offset + ahead
                    if place not in held:
                        held[place] = keep[name][index * group + offset + ahead]
                    return held[place]

                return at

            for offset in range(group):
                carry = body(index * group + offset, reader(offset), carry)
            return carry

        if not apart and group == slabs:
            return step(0, carry)
        return lax.fori_loop(0, slabs // group * once, step, carry)

    def last(name, ahead=0):
        return keep[name][slabs - 1 + ahead]

    def close(names):
        for name in names:
            keep[name][slabs] = pltpu.roll(keep[name][0], 7, 1)

    def wrapped(values):
        return tuple(pltpu.roll(value, 1, 1) for value in values)

    def down_gap(name, at):
        return at(name, 1) - at(name)

    def row_fluxes(names, at):
        weight = at("wd")
        gaps = [down_gap(name, at) for name in names]
        return gaps, tuple(weight * gap for gap in gaps)

    def spread(names, at, above):
        row_gaps, row_flux = row_fluxes(names, at)
        weight = at("wr")
        out, col_gaps = [], []
        for name, flux, before in zip(names, row_flux, above):
            value = at(name)
            gap = right(value) - value
            col_flux = weight * gap
            out.append(value + (flux - before) + (col_flux - left(col_flux)))
            col_gaps.append(gap)
        return out, row_gaps, col_gaps, row_flux

    def begin(k, at, _):
        for t in range(sum(cycles)):
            keep["half"][k, t] = 0.25 * REACH_MAX + 0.25 * REACH_MAX * jnp.tanh(0.5 * load(DISPERSAL, k, t))
            land = load(LAND, k, t)
            keep["land"][k, t] = land
            keep["rate"][k, t] = LOG2_E * land
            raw = load(SELECTION, k, t)
            keep["hs"][k, t] = 0.5 * jnp.maximum(raw, 0.0) + HALF_LN_2 * jnp.log2(1.0 + jnp.exp2(-LOG2_E * jnp.abs(raw)))
            n, z, v = load(DENSITY, k, t), load(TRAIT, k, t), load(VARIANCE, k, t)
            u = v + z * z
            keep["n0"][k, t] = n
            keep["z0"][k, t] = z
            keep["u0"][k, t] = u
            keep["q0"][k, t] = n * z
            keep["m0"][k, t] = n * u
        return ()

    each_slab(0, begin)
    close(("half", "land", "n0", "q0", "m0"))

    def weigh(k, at, _):
        half, land = at("half"), at("land")
        pair = land * at("land", 1)
        keep["ld"][k] = pair
        keep["wd"][k] = (half + at("half", 1)) * pair
        pair = land * right(land)
        keep["lr"][k] = pair
        keep["wr"][k] = (half + right(half)) * pair
        return ()

    each_slab(1, weigh)
    first_names, second_names = ("n0", "q0", "m0"), ("n1", "q1", "m1")

    def first_step(k, at, above):
        spreads, _, col_gaps, above = spread(first_names, at, above)
        for name, gap in zip(("dr0n", "dr0q", "dr0m"), col_gaps):
            keep[name][k] = gap
        for t in range(sum(cycles)):
            ns, qs, ms = (value[t] for value in spreads)
            optimum, hs = load(OPTIMUM, k, t), at("hs", tile=t)
            r = reciprocal(ns + PRIOR_WEIGHT)
            zs = (qs + PRIOR_WEIGHT * at("z0", tile=t)) * r
            es = (ms + PRIOR_WEIGHT * at("u0", tile=t)) * r
            vs = es - zs * zs
            d = zs - optimum
            misfit = d * d + vs
            p = reciprocal(1.0 + (hs + hs) * vs)
            e = jnp.exp2(at("rate", tile=t) * (GROWTH_RATE - GROWTH_RATE * ns - hs * misfit))
            n1 = ns * e
            z1 = optimum + p * d
            u1 = vs * p + MUTATION_INPUT + z1 * z1
            for name, value in zip(
                ("e", "d", "vs", "p", "zs", "es", "misfit", "r", "n1", "q1", "m1", "z1", "u1"),
                (e, d, vs, p, zs, es, misfit, r, n1, n1 * z1, n1 * u1, z1, u1),
            ):
                keep[name][k, t] = value
        return above

    each_slab(2, first_step, wrapped(row_fluxes(first_names, last)[1]))
    close(second_names)

    def second_step(k, at, above):
        spreads, _, col_gaps, above = spread(second_names, at, above)
        for name, gap in zip(("dr1n", "dr1q", "dr1m"), col_gaps):
            keep[name][k] = gap
        for t in range(sum(cycles)):
            ns, qs, ms = (value[t] for value in spreads)
            optimum, hs, land = load(OPTIMUM, k, t), at("hs", tile=t), at("land", tile=t)
            r = reciprocal(ns + PRIOR_WEIGHT)
            zs = (qs + PRIOR_WEIGHT * at("z1", tile=t)) * r
            es = (ms + PRIOR_WEIGHT * at("u1", tile=t)) * r
            vs = es - zs * zs
            d = zs - optimum
            misfit = d * d + vs
            e = jnp.exp2(at("rate", tile=t) * (GROWTH_RATE - GROWTH_RATE * ns - hs * misfit))
            n2 = ns * e
            an = jnp.where(steps_at(k, t) == 2.0, land, 0.0) * (n2 - load(OBSERVED, k, t))
            b = an * n2
            am = -(b * hs) * r
            aq = (-2.0 * optimum) * am
            keep["gsel"][k, t] = b * misfit
            keep["a2n"][k, t] = an * e - 0.5 * b - (aq * zs + am * es)
            keep["a2q"][k, t] = aq
            keep["a2m"][k, t] = am
        return above

    each_slab(3, second_step, wrapped(row_fluxes(second_names, last)[1]))
    second_back, first_back = ("a2n", "a2q", "a2m"), ("a1n", "a1q", "a1m")
    close(second_back)

    def back(k, at, above):
        spreads, row_gaps, col_gaps, above = spread(second_back, at, above)
        n_gap, q_gap, m_gap = [down_gap(name, at) * gap for name, gap in zip(second_names, row_gaps)]
        keep["gd"][k] = n_gap + q_gap + m_gap
        n_gap, q_gap, m_gap = [at(f) * gap for f, gap in zip(("dr1n", "dr1q", "dr1m"), col_gaps)]
        keep["gr"][k] = n_gap + q_gap + m_gap
        for t in range(sum(cycles)):
            an, aq, am = (value[t] for value in spreads)
            n1, z1, land, hs = at("n1", tile=t), at("z1", tile=t), at("land", tile=t), at("hs", tile=t)
            e, d, vs, p, zs, es, r = (at(name, tile=t) for name in ("e", "d", "vs", "p", "zs", "es", "r"))
            av = PRIOR_WEIGHT * at("a2m", tile=t) + am * n1
            az = PRIOR_WEIGHT * at("a2q", tile=t) + aq * n1 + (z1 + z1) * av
            an = an + aq * z1 + am * at("u1", tile=t) + jnp.where(steps_at(k, t) == 1.0, land, 0.0) * (n1 - load(OBSERVED, k, t))
            b = an * n1 * land
            bs = b * hs
            ar = (az * d + av * vs) * ((p + p) * p)
            gsel = at("gsel", tile=t) + ar * vs + b * at("misfit", tile=t)
            avs = av * p - ar * hs - bs
            azs = az * p - 2.0 * (bs * d + zs * avs)
            aqs, ams = azs * r, avs * r
            keep["a1n"][k, t] = an * e - 0.5 * b - (aqs * zs + ams * es)
            keep["a1q"][k, t] = aqs
            keep["a1m"][k, t] = ams
            raw = load(SELECTION, k, t)
            put(1, k, t, gsel * (-0.5 * LOSS_WEIGHT - 0.5 * LOSS_WEIGHT * jnp.tanh(0.5 * raw)))
        return above

    each_slab(4, back, wrapped(row_fluxes(second_back, last)[1]))
    close(first_back)

    def row_share(at):
        n_gap, q_gap, m_gap = [down_gap(a, at) * down_gap(f, at) for a, f in zip(first_back, first_names)]
        return (at("gd") + n_gap + q_gap + m_gap) * at("ld")

    def finish(k, at, above):
        here = row_share(at)
        total = at("gr")
        for name, field in zip(first_back, ("dr0n", "dr0q", "dr0m")):
            value = at(name)
            total = total + (right(value) - value) * at(field)
        total = total * at("lr")
        half = at("half")
        scale = half * (2.0 * LOSS_WEIGHT / (0.5 * REACH_MAX) * half - 2.0 * LOSS_WEIGHT)
        total = scale * (here + above[0] + total + left(total))
        for t in range(sum(cycles)):
            put(0, k, t, total[t])
        return (here,)

    each_slab(5, finish, wrapped((row_share(last),)))


def step_rows(line):
    return jnp.transpose(jnp.concatenate([line] * (LANES // 8), 0))


def tile_copies(tiles, first, rows, sources, fields, codes, sems):
    density, trait, variance, optimum, observed, land_code, maps = sources
    moves = (
        (maps, fields.at[DISPERSAL : SELECTION + 1]),
        (land_code, codes),
        (density.at[0], fields.at[DENSITY]),
        (trait.at[0], fields.at[TRAIT]),
        (variance.at[0], fields.at[VARIANCE]),
        (optimum.at[0], fields.at[OPTIMUM]),
        (observed.at[0], fields.at[OBSERVED]),
    )
    part = pl.ds(first, rows)
    copies = []
    for index, (source, target) in enumerate(moves):
        for t in range(tiles):
            lanes = pl.ds(t * LANES, LANES)
            if source is maps:
                ends = source.at[:, part, lanes], target.at[:, t, part]
            else:
                ends = source.at[part, lanes], target.at[t, part]
            copies.append(pltpu.make_async_copy(*ends, sems.at[index, t]))
    return copies


def window_kernel(first, rows, skip, fields, steps, *refs):
    out_ref, grads, kept = refs[-3:]
    tiles = fields.shape[1]
    out_rows = out_ref.shape[1]
    slabs = rows // 8

    def load(field, k, t):
        return fields[field, t, pl.ds(first + k, 8, stride=slabs), :]

    def steps_at(k, t):
        return steps[0, pl.ds(first + k, 8, stride=slabs), :]

    def put(which, k, t, value):
        grads[which, t, pl.ds(k, 8, stride=slabs), :] = value

    keep = {name: kept.at[index] for index, name in enumerate(SAVED)}
    dynamics(slabs, GROUPS[slabs], (tiles,), load, steps_at, keep, put)
    for which in range(2):
        for t in range(tiles):
            out_ref[which, :, t * LANES : (t + 1) * LANES] = grads[which, t, skip : skip + out_rows, :]


def first_kernel(tiles, rows, *refs):
    sources, step_ref = refs[:7], refs[7]
    out_ref, fields, steps, pair_ref, other_ref, codes, line, grads, kept, sems, late_sems = refs[8:]
    height = fields.shape[2]
    early = tile_copies(tiles, 0, rows, sources, fields, codes, sems)
    late = tile_copies(tiles, rows, height - rows, sources, fields, codes, late_sems)
    steps_copy = pltpu.make_async_copy(step_ref, line, sems.at[7, 0])
    for copy in [steps_copy] + early + late:
        copy.start()
    steps_copy.wait()
    wide = jnp.broadcast_to(line[0:1, :].astype(F32), (8, LANES))
    steps[0] = step_rows(wide)
    steps[1] = jnp.broadcast_to(wide[0:1], (LANES, LANES))
    for copy in early:
        copy.wait()
    fields[LAND, :, :rows] = codes[:, :rows].astype(F32)
    window_kernel(0, rows, 0, fields, steps, out_ref, grads, kept)
    for copy in late:
        copy.wait()
    fields[LAND, :, rows:] = codes[:, rows:].astype(F32)
    columns_kernel(fields, pair_ref, other_ref)


def first_window(rows, out_rows, sources, obs_step):
    height, columns = sources[0].shape[1:]
    tiles = columns // LANES
    strip = jax.ShapeDtypeStruct((FIELDS, EDGE, height), F32)
    return pl.pallas_call(
        functools.partial(first_kernel, tiles, rows),
        out_shape=[
            jax.ShapeDtypeStruct((2, out_rows, columns), F32),
            jax.ShapeDtypeStruct((FIELDS, tiles, height, LANES), F32),
            jax.ShapeDtypeStruct((2, LANES, LANES), F32),
            strip,
            strip,
        ],
        in_specs=[pl.BlockSpec(memory_space=pltpu.HBM)] * 8,
        out_specs=[pl.BlockSpec(memory_space=pltpu.VMEM)] * 5,
        scratch_shapes=[
            pltpu.VMEM((tiles, height, LANES), jnp.int32),
            pltpu.VMEM(obs_step.shape, jnp.int32),
            pltpu.VMEM((2, tiles, rows, LANES), F32),
            pltpu.VMEM((len(SAVED), rows // 8 + 1, tiles, 8, LANES), F32),
            pltpu.SemaphoreType.DMA((8, tiles)),
            pltpu.SemaphoreType.DMA((7, tiles)),
        ],
        cost_estimate=cost(WINDOW_US),
        compiler_params=pltpu.CompilerParams(vmem_limit_bytes=VMEM_BYTES),
        name="first_window",
    )(*(pltpu.with_memory_space_constraint(source, pltpu.HBM) for source in (*sources, obs_step)))


def window(first, rows, out_first, out_rows, fields, steps, *after):
    tiles = fields.shape[1]
    return pl.pallas_call(
        functools.partial(window_kernel, first, rows, out_first - first),
        out_shape=jax.ShapeDtypeStruct((2, out_rows, tiles * LANES), F32),
        in_specs=[pl.BlockSpec(memory_space=pltpu.VMEM)] * 2 + [pl.BlockSpec(memory_space=pltpu.VMEM)] * len(after),
        out_specs=pl.BlockSpec(memory_space=pltpu.VMEM),
        scratch_shapes=[
            pltpu.VMEM((2, tiles, rows, LANES), F32),
            pltpu.VMEM((len(SAVED), rows // 8 + 1, tiles, 8, LANES), F32),
        ],
        cost_estimate=cost(WINDOW_US),
        compiler_params=pltpu.CompilerParams(vmem_limit_bytes=VMEM_BYTES),
        name=f"window_{out_first}",
    )(fields, steps, *after)


def columns_kernel(fields, pair_ref, other_ref):
    rightward = is_even("ly")
    tiles, rows = fields.shape[1:3]
    lane = lax.broadcasted_iota(jnp.int32, (rows, LANES), 1)
    packed = jnp.zeros((rows, LANES), F32)
    for field in range(FIELDS):
        both = jnp.where(lane < EDGE, fields[field, 0], fields[field, tiles - 1])
        turned = pltpu.roll(both, 16 * field, 1) if field else both
        place = (lane - 16 * field + EDGE) % LANES
        packed = jnp.where(place < 2 * EDGE, turned, packed)
    flipped = jnp.transpose(packed)
    for field in range(FIELDS):
        left = flipped[16 * field : 16 * field + EDGE]
        start = (16 * field - EDGE) % LANES
        right = flipped[start : start + EDGE]
        pair_ref[field] = jnp.where(rightward, right, left)
        other_ref[field] = jnp.where(rightward, left, right)


def in_vmem(kernel, name, out_shape):
    def call(*operands):
        many = isinstance(out_shape, (list, tuple))
        space = pl.BlockSpec(memory_space=pltpu.VMEM)
        return pl.pallas_call(
            kernel,
            out_shape=out_shape,
            in_specs=[space] * len(operands),
            out_specs=[space] * len(out_shape) if many else space,
            compiler_params=pltpu.CompilerParams(vmem_limit_bytes=VMEM_BYTES),
            name=name,
        )(*operands)

    return call


def is_even(axis):
    return lax.axis_index(axis) % 2 == 0


def present(axis):
    place = lax.axis_index(axis)
    return (place > 0).astype(F32), (place < lax.axis_size(axis) - 1).astype(F32)


def chosen(which, one, other):
    return lambda index: jnp.where(which, one[index], other[index])


def rows_kernel(fields, steps, from_pair, from_other, pair_ref, other_ref):
    tiles = fields.shape[1]
    downward, rightward = is_even("lx"), is_even("ly")
    sub = lax.broadcasted_iota(jnp.int32, (8, LANES), 0)
    for pair in range(FIELDS // 2):
        for t in range(tiles):
            even, odd = fields.at[2 * pair, t], fields.at[2 * pair + 1, t]
            up = jnp.where(sub < HALO, even[:EDGE], pltpu.roll(odd[:EDGE], HALO, 0))
            down = jnp.where(sub < HALO, pltpu.roll(odd[-EDGE:], HALO, 0), even[-EDGE:])
            pair_ref[pair * tiles + t] = jnp.where(downward, down, up)
            other_ref[pair * tiles + t] = jnp.where(downward, up, down)
    lane = lax.broadcasted_iota(jnp.int32, (8, LANES), 1)
    base = FIELDS // 2 * tiles
    strips = chosen(rightward, from_other, from_pair), chosen(rightward, from_pair, from_other)
    for index, strip in enumerate(strips):
        packed = jnp.zeros((8, LANES), F32)
        for field in range(FIELDS):
            turned = pltpu.roll(strip(field), 8 * field, 1) if field else strip(field)
            place = (lane - 8 * field + HALO) % LANES
            packed = jnp.where(place < 2 * HALO, turned, packed)
        pair_ref[base + index] = packed
        other_ref[base + index] = packed
    pair_ref[base + 2] = steps[1, :8]
    other_ref[base + 2] = steps[1, :8]


def pack_rows(*operands):
    fields = operands[0]
    shape = jax.ShapeDtypeStruct((FIELDS // 2 * fields.shape[1] + 3, 8, LANES), F32)
    return in_vmem(rows_kernel, "pack_rows", [shape, shape])(*operands)


def outer_rows(grad, which, t):
    sub = lax.broadcasted_iota(jnp.int32, (8, LANES), 0)
    return jnp.where(sub < HALO, grad[which, t, 8:16, :], grad[which, t, 16:24, :])


def edges_kernel(fields, steps, own_pair, own_other, side_pair, side_other, end_pair, end_other, *refs):
    out_ref, strip, grad, kept, row_step = refs
    tiles = fields.shape[1]
    base = FIELDS // 2 * tiles
    (has_above, has_below), (has_left, has_right) = present("lx"), present("ly")
    downward, rightward = is_even("lx"), is_even("ly")
    own_left, own_right = chosen(rightward, own_other, own_pair), chosen(rightward, own_pair, own_other)
    from_left, from_right = chosen(rightward, side_other, side_pair), chosen(rightward, side_pair, side_other)
    from_above, from_below = chosen(downward, end_other, end_pair), chosen(downward, end_pair, end_other)
    lane = lax.broadcasted_iota(jnp.int32, (8, LANES), 1)
    sub = lax.broadcasted_iota(jnp.int32, (8, LANES), 0)
    within = jnp.where(lane < LANES // 2, has_below, has_above)

    def lined(value, outer):
        out = jnp.where(lane < 8, pltpu.roll(outer, 8, 1), pltpu.roll(value, 8, 1))
        out = jnp.where(lane < 16, out, pltpu.roll(value, 24, 1))
        return jnp.where(lane < 24, out, pltpu.roll(outer, 24, 1))

    def beside(side, index, present):
        corners = jnp.where((lane % 8) < HALO, from_below(base + index), from_above(base + index))
        out = []
        for field in range(FIELDS):
            value = side(field)
            outer = pltpu.roll(corners, (LANES - 8 * field) % LANES, 1) if field else corners
            if field == LAND:
                value, outer = value * present, outer * (within * present)
            out.append(lined(value, outer))
        return out

    lefts, rights = beside(from_left, 0, has_left), beside(from_right, 1, has_right)
    zeros = jnp.zeros((8, LANES), F32)
    stack = []
    for index in range(LANES // 8):
        following = (index + 1) % (LANES // 8)
        here = rights[index] if index < FIELDS else zeros
        after = lefts[following] if following < FIELDS else zeros
        stack.append(jnp.where(sub < HALO, here, after))
    outer_step = jnp.where(lane < LANES // 2, from_below(base + 2), from_above(base + 2))
    stack[FIELDS] = lined(steps[1, :8], outer_step)
    flipped = jnp.transpose(jnp.concatenate(stack, 0))[:32]
    row_step[...] = jnp.broadcast_to(flipped[:, 8 * FIELDS : 8 * FIELDS + 1], (32, LANES))
    for field in range(FIELDS):
        for t in range(tiles):
            above, below = from_above(field // 2 * tiles + t), from_below(field // 2 * tiles + t)
            if field % 2:
                above, below = pltpu.roll(above, HALO, 0), pltpu.roll(below, HALO, 0)
            if field == LAND:
                above, below = above * has_above, below * has_below
            own = fields.at[field, t]
            for index, value in enumerate((above, own[:EDGE], own[-EDGE:], below)):
                strip[field, t, 8 * index : 8 * index + 8, :] = value
        strip[field, tiles] = pltpu.roll(flipped, (LANES - 8 * field) % LANES, 1) if field else flipped
        left, right = from_left(field), from_right(field)
        if field == LAND:
            left, right = left * has_left, right * has_right
        for index, value in enumerate((left, own_left(field), own_right(field), right)):
            strip[field, tiles + 1, 8 * index : 8 * index + 8, :] = value

    slabs = 3
    count = tiles + 2

    def load(field, k, t):
        return strip[field, t, pl.ds(HALO + k, 8, stride=slabs), :]

    def steps_at(k, t):
        return row_step[pl.ds(HALO + k, 8, stride=slabs), :] if t <= tiles else steps[1, :8]

    def put(which, k, t, value):
        grad[which, t, pl.ds(HALO + k, 8, stride=slabs), :] = value

    keep = {name: kept.at[index] for index, name in enumerate(SAVED)}
    dynamics(slabs, (slabs,) * 6, (tiles + 1, 1), load, steps_at, keep, put)
    for which in range(2):
        for t in range(tiles):
            out_ref[which, :, t * LANES : (t + 1) * LANES] = outer_rows(grad, which, t)
        out_ref[which, :, tiles * LANES :] = outer_rows(grad, which, tiles + 1)


def edges(fields, steps, *strips):
    tiles = fields.shape[1]
    count = tiles + 2
    space = pl.BlockSpec(memory_space=pltpu.VMEM)
    operands = [fields, steps, *strips]
    return pl.pallas_call(
        edges_kernel,
        out_shape=jax.ShapeDtypeStruct((2, EDGE, (tiles + 1) * LANES), F32),
        in_specs=[space] * len(operands),
        out_specs=space,
        scratch_shapes=[
            pltpu.VMEM((FIELDS, count, 32, LANES), F32),
            pltpu.VMEM((2, count, 32, LANES), F32),
            pltpu.VMEM((len(SAVED), 4, count, 8, LANES), F32),
            pltpu.VMEM((32, LANES), F32),
        ],
        cost_estimate=cost(EDGES_US),
        compiler_params=pltpu.CompilerParams(vmem_limit_bytes=VMEM_BYTES),
        name="edges",
    )(*operands)


def update_kernel(parts, terms, maps_ref, first_ref, second_ref, *refs):
    grads, edge_refs = refs[: parts * terms], refs[parts * terms : (parts + 1) * terms]
    new_maps, new_first, new_second = refs[(parts + 1) * terms :]
    rows, columns = maps_ref.shape[1:]
    tiles = columns // LANES
    lane = lax.broadcasted_iota(jnp.int32, (rows, LANES), 1)
    sub = lax.broadcasted_iota(jnp.int32, (EDGE, LANES), 0)
    edge = sum(ref[...] for ref in edge_refs)
    strips = [edge[which, :, columns:] for which in range(2)]
    blank = jnp.zeros((LANES - 2 * EDGE, LANES), F32)
    flipped = jnp.transpose(jnp.concatenate([*strips, blank], 0))
    for which in range(2):
        for t in range(tiles):
            own = slice(t * LANES, (t + 1) * LANES)
            grad = jnp.concatenate(
                [sum(ref[which, :, own] for ref in grads[part * terms : (part + 1) * terms]) for part in range(parts)],
                0,
            )
            if t == 0:
                beside = pltpu.roll(flipped, LANES - EDGE * which, 1) if which else flipped
                grad = jnp.where(lane < HALO, beside, grad)
            if t == tiles - 1:
                beside = pltpu.roll(flipped, LANES - EDGE * (which + 1), 1)
                grad = jnp.where(lane >= LANES - HALO, beside, grad)
            outer = edge[which, :, own]
            grad = jnp.concatenate(
                [
                    jnp.where(sub < HALO, outer, grad[:EDGE]),
                    grad[EDGE:-EDGE],
                    jnp.where(sub < HALO, grad[-EDGE:], outer),
                ],
                0,
            )
            first = BETA_FIRST * first_ref[which, :, own] + (1.0 - BETA_FIRST) * grad
            second = BETA_SECOND * second_ref[which, :, own] + (1.0 - BETA_SECOND) * grad * grad
            new_first[which, :, own] = first
            new_second[which, :, own] = second
            scale = jnp.sqrt(second * (1.0 / (1.0 - BETA_SECOND**ADAM_STEP))) + ADAM_EPS
            change = (LEARN_RATE / (1.0 - BETA_FIRST**ADAM_STEP)) * first
            new_maps[which, :, own] = maps_ref[which, :, own] - change * reciprocal(scale)


def update(maps, first_moment, second_moment, grads, edge_grads):
    parts, terms = len(grads), len(edge_grads)
    flat = [term for grad in grads for term in grad]
    shape = jax.ShapeDtypeStruct(maps.shape, F32)
    kernel = functools.partial(update_kernel, parts, terms)
    return in_vmem(kernel, "update", [shape] * 3)(maps, first_moment, second_moment, *flat, *edge_grads)


def swapped(arrays, axis, other):
    count, beside, columns = lax.axis_size(axis), lax.axis_size(other), lax.axis_size("ly")
    out = []
    for array, start in zip(arrays, (0, 1)):
        swaps = [(i, i + 1) for i in range(start, count - 1, 2)]
        alone = sorted(set(range(count)) - {i for swap in swaps for i in swap})
        pairs = [((i, k), (j, k)) for i, j in swaps for k in range(beside)]
        if ENDS_MEET[axis] and len(alone) == 2:
            pairs += [((alone[0], k), (alone[1], k)) for k in range(beside)]
        else:
            pairs += [((i, k), (i, k + 1)) for i in alone for k in range(0, beside - 1, 2)]
        if axis == "ly":
            pairs = [tuple(place[::-1] for place in pair) for pair in pairs]
        flat = [tuple(row * columns + column for row, column in pair) for pair in pairs]
        out.append(lax.ppermute(array, ("lx", "ly"), flat + [pair[::-1] for pair in flat]))
    return out


def both_scenarios(value):
    count = lax.axis_size("scen")
    if count == 2:
        return [value, lax.ppermute(value, "scen", [(0, 1), (1, 0)])]
    return [lax.psum(value, "scen")]


def shards(
    density,
    trait,
    variance,
    optimum,
    observed,
    obs_step,
    land_code,
    maps,
    first_moment,
    second_moment,
):
    sources = (density, trait, variance, optimum, observed, land_code, maps)
    rows = maps.shape[1]
    upper, fields, steps, *own_sides = first_window(CUTS[0] + EDGE, CUTS[0], sources, obs_step)
    upper_terms = both_scenarios(upper)
    sides = swapped(own_sides, "ly", "lx")
    middle = window(CUTS[0] - HALO, CUTS[1] - CUTS[0] + EDGE, CUTS[0], CUTS[1] - CUTS[0], fields, steps, *own_sides)
    middle_terms = both_scenarios(middle)
    own_ends = pack_rows(fields, steps, *sides)
    ends = swapped(own_ends, "lx", "ly")
    last = rows - CUTS[1]
    after = *own_sides, *sides, *own_ends, upper_terms[-1]
    lower = window(CUTS[1] - EDGE, last + EDGE, CUTS[1], last, fields, steps, *after)
    lower_terms = both_scenarios(lower)
    outer = edges(fields, steps, *own_sides, *sides, *ends)
    outer_terms = both_scenarios(outer)
    return tuple(update(maps, first_moment, second_moment, [upper_terms, middle_terms, lower_terms], outer_terms))


def solution(mesh):
    in_specs = (
        P("scen", "lx", "ly"),
        P("scen", "lx", "ly"),
        P("scen", "lx", "ly"),
        P("scen", "lx", "ly"),
        P("scen", "lx", "ly"),
        P("scen", "lx"),
        P("lx", "ly"),
        P(None, "lx", "ly"),
        P(None, "lx", "ly"),
        P(None, "lx", "ly"),
    )
    out_specs = (P(None, "lx", "ly"), P(None, "lx", "ly"), P(None, "lx", "ly"))
    return jax.shard_map(shards, mesh=mesh, in_specs=in_specs, out_specs=out_specs, check_vma=False)
```
